512 devices in a mesh: loop: 64 (over z, y_hi, core), rep: 8 (over y_lo, x).
Axes of the slice: x: 4, y: 8 (y_hi: 4, y_lo: 2; y = y_hi * 2 + y_lo), z: 8, core: 2. Of those that a mesh axis runs over, the one named last changes fastest.
Arguments:
- node_feats: bfloat16 [32768, 256], P(('loop', 'rep')), may hold values from -6 to 6
- weight_matrix: bfloat16 [256, 256], replicated, may hold values from -0.375 to 0.375
- tile_values: bfloat16 [32768, 128, 128], P(('loop', 'rep')), may hold values from -0.25 to 0.25
- tile_rows: int32 [32768], P(('loop', 'rep')), may hold values from 0 to 3, as said below
- tile_cols: int32 [32768], P(('loop', 'rep')), may hold values from 0 to 31
- tile_count: int32 [512], P(('loop', 'rep')), may hold values from 1 to 64, as said below
- labelled: int32 [64, 32], P('loop'), may hold values from 0 to 511
- upstream: bfloat16 [32768, 256], P('loop'), may hold values from -6 to 6
Outputs:
- layer_out: bfloat16 [32768, 256], P(('loop', 'rep'))
- grad_feats: bfloat16 [32768, 256], P(('loop', 'rep'))
- grad_weight: float32 [256, 256], replicated
The draws below stay inside these ranges and needn't reach their ends.
Inputs may be any that keep to these rules, and one draw needn't show every extreme that they name: On each device the first tile_count slots name distinct (tile_rows, tile_cols) positions; later slots are unused. `tile_count`: some device has all 64 slots live.
All inputs are finite; a program needn't handle non-finite values.
Results may differ from the reference program's by a relative error of at most 0.0061.
Values may be sent and summed in bfloat16 or wider, within the bound.
A program may use at most 64 MiB of HBM per device.

```python
import jax
import jax.numpy as jnp
from jax import lax

FEAT = 256
ROWS_DEV = 64
LAB_TEAM = 32
TILE = 128
NODES = 32768
TEAMS = 64
BLOCK_ROWS = 512
RTILES = 4
CTILES = 32
TILES_DEV = 64
SLOTS = 32768
N_LOOP = 64
N_REP = 8


def tile_positions(key):
    device_total = SLOTS // TILES_DEV
    device_keys = jax.random.split(key, device_total)

    def pick_device(device_key):
        return jax.random.permutation(device_key, RTILES * CTILES)[:TILES_DEV]
    return jax.vmap(pick_device)(device_keys).astype(jnp.int32)


def relabel(key, index_table, count):
    device_total = SLOTS // TILES_DEV
    device_keys = jax.random.split(key, device_total)

    def one_device(device_key, indices):
        order = jax.random.permutation(device_key, count).astype(jnp.int32)
        return order[indices]
    return jax.vmap(one_device)(device_keys, index_table).reshape(SLOTS).astype(jnp.int32)


def draw_tile_rows(key, part):
    spots = tile_positions(key)
    key = jax.random.fold_in(key, 3)
    return relabel(key, (spots // CTILES).astype(jnp.int32), RTILES)


def draw_tile_cols(key, part):
    spots = tile_positions(key)
    key = jax.random.fold_in(key, 4)
    return relabel(key, (spots % CTILES).astype(jnp.int32), CTILES)


def draw_tile_count(key, part):
    key = jax.random.fold_in(key, 5)
    first_key, second_key, third_key = jax.random.split(key, 3)
    device_total = SLOTS // TILES_DEV
    first_draw = jax.random.randint(first_key, (device_total,), 0, TILES_DEV)
    second_draw = jax.random.randint(second_key, (device_total,), 0, TILES_DEV)
    counts = 1 + first_draw * second_draw // TILES_DEV
    chosen = jax.random.randint(third_key, (), 0, device_total)
    return jnp.where(jnp.arange(device_total) == chosen, TILES_DEV, counts).astype(jnp.int32)


def with_ends(array, key, smallest, largest):
    place = [jax.random.randint(jax.random.fold_in(key, axis), (), 0, length) for axis, length in enumerate(array.shape)]
    longest = array.shape.index(max(array.shape))
    beside = place[:longest] + [(place[longest] + 1) % array.shape[longest]] + place[longest + 1:]
    return array.at[tuple(place)].set(smallest).at[tuple(beside)].set(largest)


def level_of(rng, dims, cuts, smallest, largest):
    gain, own = 1.0, jax.random.fold_in(rng, 6)
    for position, blocks in cuts:
        draws = jnp.exp(jax.random.uniform(jax.random.fold_in(own, position), (blocks,), jnp.float32, smallest / len(cuts), largest / len(cuts)))
        gain = gain * jnp.repeat(draws, dims[position] // blocks).reshape([-1 if axis == position else 1 for axis in range(len(dims))])
    return gain


def noise(own_key, dims, deviation, limit, shards=(), kind=jnp.bfloat16):
    array = jax.random.normal(own_key, dims, jnp.float32) * deviation
    if len(shards) > 0:
        array = level_of(own_key, dims, shards, -0.22, 0.18) * array
    return jnp.clip(array, min=-limit, max=limit).astype(kind)


def setup_inputs(seed: int = 0) -> dict:
    arg_keys = jax.random.split(jax.random.key(seed), 9)
    return {
        "node_feats": noise(arg_keys[0], (NODES, FEAT), 1.0, 6.0, ((0, 512),)),
        "weight_matrix": noise(arg_keys[1], (FEAT, FEAT), FEAT ** -0.5, 0.375),
        "tile_values": noise(arg_keys[2], (SLOTS, TILE, TILE), (0.2 / TILE ** 0.5), 0.25, ((0, 512),)),
        "tile_rows": draw_tile_rows(jax.random.fold_in(arg_keys[8], 71), 0),
        "tile_cols": draw_tile_cols(jax.random.fold_in(arg_keys[8], 71), 0),
        "tile_count": draw_tile_count(jax.random.fold_in(arg_keys[8], 71), 0),
        "labelled": with_ends(jax.random.randint(arg_keys[6], (TEAMS, LAB_TEAM), 0, BLOCK_ROWS), jax.random.fold_in(arg_keys[6], 1), 0, BLOCK_ROWS - 1).astype(jnp.int32),
        "upstream": noise(arg_keys[7], (NODES, FEAT), 1.0, 6.0, ((0, 64),)),
    }


def silu_pair(pre_act):
    gate_value = jax.nn.sigmoid(pre_act)
    return pre_act * gate_value, gate_value * (1.0 + pre_act * (1.0 - gate_value))


def reference(node_feats, weight_matrix, tile_values, tile_rows, tile_cols, tile_count, labelled, upstream):
    width = node_feats.shape[1]
    block_rows = ROWS_DEV * N_REP
    group = node_feats.reshape(N_LOOP, N_REP, ROWS_DEV, width).transpose(1, 0, 2, 3).reshape(N_REP, CTILES, TILE, width)
    team_values = tile_values.reshape(N_LOOP, N_REP, TILES_DEV, TILE, TILE)
    team_rows = tile_rows.reshape(N_LOOP, N_REP, TILES_DEV)
    team_cols = tile_cols.reshape(N_LOOP, N_REP, TILES_DEV)
    team_live = jnp.arange(TILES_DEV, dtype=jnp.int32)[None, None, :] < tile_count.reshape(N_LOOP, N_REP)[:, :, None]
    rep_ids = jnp.arange(N_REP, dtype=jnp.int32)[:, None]

    def team_forward(inputs):
        values, row_ids, col_ids, alive = inputs
        masked = jnp.where(alive[:, :, None, None], values.astype(jnp.float32), jnp.float32(0.0))
        source = group[rep_ids, col_ids].astype(jnp.float32)
        product = jnp.einsum("rkij,rkjf->rkif", masked, source)
        onehot = (row_ids[:, :, None] == jnp.arange(RTILES, dtype=jnp.int32)[None, None, :]).astype(jnp.float32)
        return jnp.einsum("rkt,rkif->tif", onehot, product)

    aggregate = lax.map(team_forward, (team_values, team_rows, team_cols, team_live)).reshape(NODES, width)
    aggregate_low = aggregate.astype(jnp.bfloat16)
    pre_act = jnp.dot(aggregate_low, weight_matrix, preferred_element_type=jnp.float32)
    activated, slope = silu_pair(pre_act)
    layer_out = activated.astype(jnp.bfloat16)
    label_rows = jnp.any(labelled[:, :, None] == jnp.arange(block_rows, dtype=jnp.int32)[None, None, :], axis=1)
    mask = label_rows.reshape(NODES).astype(jnp.float32)
    grad_pre = (upstream.astype(jnp.float32) * slope * mask[:, None]).astype(jnp.bfloat16)
    grad_weight = jnp.dot(aggregate_low.T, grad_pre, preferred_element_type=jnp.float32)
    grad_agg = jnp.dot(grad_pre, weight_matrix.T, preferred_element_type=jnp.float32).astype(jnp.bfloat16)
    grad_agg = grad_agg.reshape(N_LOOP, RTILES, TILE, width)

    def team_backward(total, inputs):
        values, row_ids, col_ids, alive, team_grad = inputs
        masked = jnp.where(alive[:, :, None, None], values.astype(jnp.float32), jnp.float32(0.0))
        source = team_grad[row_ids].astype(jnp.float32)
        product = jnp.einsum("rkij,rkif->rkjf", masked, source)
        onehot = (col_ids[:, :, None] == jnp.arange(CTILES, dtype=jnp.int32)[None, None, :]).astype(jnp.float32)
        return total + jnp.einsum("rkc,rkjf->rcjf", onehot, product), None

    start_total = jnp.zeros((N_REP, CTILES, TILE, width), jnp.float32)
    column_total, unused = lax.scan(team_backward, start_total, (team_values, team_rows, team_cols, team_live, grad_agg))
    grad_feats = column_total.reshape(N_REP, N_LOOP, ROWS_DEV, width).transpose(1, 0, 2, 3).reshape(NODES, width)
    return layer_out, grad_feats.astype(jnp.bfloat16), grad_weight
```

```python
import jax
import jax.numpy as jnp
from jax import lax
from jax.experimental import pallas as pl
from jax.experimental.pallas import tpu as pltpu
from jax.sharding import PartitionSpec as P

MESH = pl.DeviceIdType.MESH
NZ, NY, NC, NR = 8, 4, 2, 8
ROWS, FEAT, TILE, SLOTS = 64, 256, 128, 64
TEAM, LAB, RT = 512, 32, 4
COLS = NZ * NY
F32, BF16, I32 = jnp.float32, jnp.bfloat16, jnp.int32
CONTRACT_ROWS = (((0,), (0,)), ((), ()))
CONTRACT_LANES = (((1,), (1,)), ((), ()))


def iota(shape, dim):
    return lax.broadcasted_iota(I32, shape, dim)


def to_column(row):
    n = row.shape[1]
    square = jnp.broadcast_to(row, (n, n))
    return jnp.sum(jnp.where(iota((n, n), 0) == iota((n, n), 1), square, 0), axis=1, keepdims=True)


def kernel(
    feats, weight, values, trows, tcols, tcount, lab, upstream,
    layer_out, grad_feats, grad_weight,
    x3, tiles, dense, wv, upv, table_v, table_s, acc, asub, a4, at4, at8,
    stage, rep_in, msg, wpart, cstage, cin, gwbuf,
    local_sem, y_s, y_r, z_s, z_r, c_s, c_r, a_s, a_r, t_s, t_r,
    rep_s, rep_r, m_s, m_r, w_s, w_r, b_s, b_r, v_s, v_r,
):
    loop, rep = lax.axis_index("loop"), lax.axis_index("rep")
    z, yh, c = loop // 8, (loop // 2) % 4, loop % 2

    def at(dz=0, dy=0, dc=0, dr=0):
        nz, ny = lax.rem(z + dz + NZ, NZ), lax.rem(yh + dy + NY, NY)
        nc, nr = lax.rem(c + dc, NC), lax.rem(rep + dr, NR)
        return (nz * 8 + ny * 2 + nc, nr)

    sends = []

    def push(src, dst, ss, rs, to):
        copy = pltpu.make_async_remote_copy(
            src_ref=src, dst_ref=dst, send_sem=ss, recv_sem=rs, device_id=to, device_id_type=MESH
        )
        copy.start()
        sends.append(copy)
        return copy

    loads = [
        pltpu.make_async_copy(values, tiles.at[pl.ds(0, SLOTS)], local_sem.at[0]),
        pltpu.make_async_copy(feats, x3.at[z * NY + yh, pl.ds(c * ROWS, ROWS)], local_sem.at[1]),
        pltpu.make_async_copy(weight, wv, local_sem.at[2]),
        pltpu.make_async_copy(upstream, upv, local_sem.at[3]),
    ]
    for load in loads:
        load.start()

    peers = [at(dz=i) for i in range(1, NZ)]
    peers += [at(dy=i, dc=k) for k in range(2) for i in range(NY) if i + k]
    peers += [at(dr=i) for i in range(1, NR)]
    barrier = pltpu.get_barrier_semaphore()
    for peer in peers:
        pl.semaphore_signal(barrier, inc=1, device_id=peer, device_id_type=MESH)

    pos = to_column(trows[...] * COLS + tcols[...])
    live = iota((SLOTS, 1), 0) < tcount[0, 0]
    hit = (pos == iota((SLOTS, TILE), 1)) & live
    table_v[...] = SLOTS + jnp.sum(jnp.where(hit, iota((SLOTS, TILE), 0) - SLOTS, 0), axis=0, keepdims=True)
    table_copy = pltpu.make_async_copy(table_v, table_s, local_sem.at[4])
    table_copy.start()

    pl.semaphore_wait(barrier, len(peers))

    def shard(dz, dy):
        nz, ny = lax.rem(z + dz + NZ, NZ), lax.rem(yh + dy + NY, NY)
        return x3.at[nz * NY + ny, pl.ds(c * ROWS, ROWS)]

    own = shard(0, 0)
    y_in, up_in, down_in, sib_in = {}, {}, {}, {}
    for jj in (2, 1, 3):
        y_in[jj] = push(feats, own, y_s.at[jj], y_r.at[jj], at(dy=jj))

    def forward(src, block, s, jj):
        pass

    def send_up(src, s, jj):
        up_in[s, jj] = push(src, shard(1 - s, -jj), z_s.at[0, s, jj], z_r.at[0, s, jj], at(dz=1))

    def send_down(src, s, jj):
        down_in[s, jj] = push(src, shard(s - 1, -jj), z_s.at[1, s, jj], z_r.at[1, s, jj], at(dz=-1))

    def send_sib(src, dz, jj):
        i = (dz % NZ) * NY + jj
        sib_in[dz, jj] = push(src, shard(dz, -jj), c_s.at[i], c_r.at[i], at(dc=1))

    send_up(feats, 1, 0)
    send_down(feats, 1, 0)
    send_sib(feats, 0, 0)

    lab_row = lab[...]
    lab_col = to_column(lab_row)
    twice = (lab_col == lab_row) & (iota((LAB, LAB), 1) < iota((LAB, LAB), 0))
    first = jnp.sum(jnp.where(twice, 1, 0), axis=1, keepdims=True) == 0
    pick = jnp.where((lab_col == iota((LAB, TEAM), 1)) & first, 1.0, 0.0).astype(BF16)

    tiles[SLOTS] = jnp.zeros((TILE, TILE), BF16)
    table_copy.wait()
    loads[0].wait()

    def densify(nz, carry):
        for j in range(NY):
            for rt in range(RT):
                slot = table_s[0, rt * COLS + nz * NY + j]
                dense[nz, rt * TILE:(rt + 1) * TILE, j * TILE:(j + 1) * TILE] = tiles[slot]
        rows = jnp.dot(pick, dense[nz], preferred_element_type=F32).astype(BF16)
        for j in range(NY):
            asub[j, nz] = rows[:, j * TILE:(j + 1) * TILE]
        return carry

    lax.fori_loop(0, NZ, densify, 0)
    a_in = {}
    for jj in (2, 1, 3):
        a_in[jj] = push(asub.at[lax.rem(yh + jj, NY)], a4.at[yh], a_s.at[jj], a_r.at[jj], at(dy=jj))
    a4[yh] = asub[yh]

    for jj in (1, 3, 2):
        y_in[jj].wait_recv()
        src = shard(0, -jj)
        send_up(src, 1, jj)
        send_down(src, 1, jj)
        send_sib(src, 0, jj)
    loads[1].wait()

    order = (0, 1, 3, 2)

    def add_block(dz, fresh=False):
        for jj in range(NY):
            sib_in[dz, jj].wait_recv()
        nz = lax.rem(z + dz + NZ, NZ)
        block = x3[pl.ds(nz * NY, NY)].reshape(NY * TILE, FEAT)
        term = jnp.dot(dense[nz], block, preferred_element_type=F32)
        if fresh:
            acc[...] = term
        else:
            acc[...] += term

    for s in range(1, 4):
        for jj in order:
            up_in[s, jj].wait_recv()
            src = shard(-s, -jj)
            if s < 3 or jj in (0, 1):
                send_up(src, s + 1, jj)
            send_sib(src, -s, jj)
            down_in[s, jj].wait_recv()
            src = shard(s, -jj)
            if s < 3 or jj in (2, 3):
                send_down(src, s + 1, jj)
            send_sib(src, s, jj)
        if s == 1:
            add_block(0, fresh=True)
            for jj in range(1, NY):
                a_in[jj].wait_recv()
            for i in range(NZ):
                block = jnp.concatenate([a4[j, i] for j in range(NY)], axis=0)
                at4[i] = block.astype(F32).T.astype(BF16)
            t_in = push(
                at4.at[:, pl.ds((1 - c) * ROWS, ROWS)], at8.at[:, :, pl.ds(c * TILE, TILE)],
                t_s.at[0], t_r.at[0], at(dc=1),
            )
            at8[:, :, pl.ds(pl.multiple_of(c * TILE, TILE), TILE)] = at4[:, pl.ds(pl.multiple_of(c * ROWS, ROWS), ROWS)]
        else:
            add_block(1 - s)
            add_block(s - 1)
    for jj in order:
        (up_in if jj in (0, 1) else down_in)[4, jj].wait_recv()
        send_sib(shard(-4, -jj), -4, jj)
    add_block(-3)
    add_block(3)
    add_block(-4)

    low = acc[...].astype(BF16)
    picked = jnp.dot(pick, low, preferred_element_type=F32).astype(BF16)
    for i in range(NR):
        stage[i, 0:ROWS] = low[i * ROWS:(i + 1) * ROWS]
        stage[i, ROWS:ROWS + LAB] = picked
    rep_in_c = {}
    for d in (6, 2, 5, 7, 3, 1, 4):
        rep_in_c[d] = push(stage.at[lax.rem(rep + d, NR)], rep_in.at[d], rep_s.at[d], rep_r.at[d], at(dr=d))
    loads[2].wait()
    loads[3].wait()
    w = wv[...]
    up_lab = jnp.dot(pick, upv[...], preferred_element_type=F32)
    total = stage[rep].astype(F32)
    for d in (4, 1, 3, 7, 5, 2, 6):
        rep_in_c[d].wait_recv()
        total += rep_in[d].astype(F32)
    agg = total.astype(BF16)
    pre = jnp.dot(agg, w, preferred_element_type=F32)
    gate = jax.nn.sigmoid(pre)
    layer_out[...] = (pre * gate)[0:ROWS].astype(BF16)
    pre_l, gate_l = pre[ROWS:], gate[ROWS:]
    slope = gate_l * (1.0 + pre_l * (1.0 - gate_l))
    mine = c * NY + yh
    msg[mine, :, 0:FEAT] = (up_lab * slope).astype(BF16)
    chunk = (iota((FEAT, TILE), 0) == rep * LAB + iota((FEAT, TILE), 1)) & (iota((FEAT, TILE), 1) < LAB)
    msg[mine, :, FEAT:] = jnp.dot(
        agg[ROWS:], jnp.where(chunk, 1.0, 0.0).astype(BF16), preferred_element_type=F32
    ).astype(BF16)
    m_in = []
    for dy, dc in ((2, 1), (2, 0), (1, 1), (3, 1), (1, 0), (3, 0), (0, 1)):
        i = dc * NY + dy
        m_in.append(push(msg.at[mine], msg.at[mine], m_s.at[i], m_r.at[i], at(dy=dy, dc=dc)))
    t_in.wait_recv()
    for copy in reversed(m_in):
        copy.wait_recv()

    grad_pre = msg[:, :, 0:FEAT].reshape(NC * NY * LAB, FEAT)
    agg_chunk = msg[:, :, FEAT:].reshape(NC * NY * LAB, TILE)
    part = lax.dot_general(agg_chunk, grad_pre, CONTRACT_ROWS, preferred_element_type=F32)
    wpart[z] = part[0:LAB].astype(BF16)
    w_in, b_in = [], []
    for d in (4, 3, 5, 2, 6, 1, 7):
        w_in.append(push(wpart.at[z], wpart.at[z], w_s.at[d], w_r.at[d], at(dz=d)))
    grad_agg = lax.dot_general(grad_pre, w, CONTRACT_LANES, preferred_element_type=F32).astype(BF16)
    term = jnp.dot(at8[...].reshape(NZ * ROWS, NC * NY * LAB), grad_agg, preferred_element_type=F32)
    cstage[...] = term.astype(BF16).reshape(NZ, ROWS, FEAT)
    for d in (4, 3, 5, 2, 6, 1, 7):
        b_in.append(push(cstage.at[lax.rem(z + d, NZ)], cin.at[d], b_s.at[d], b_r.at[d], at(dz=d)))
    for copy in reversed(w_in):
        copy.wait_recv()
    chunk_sum = wpart[0].astype(F32)
    for i in range(1, NZ):
        chunk_sum += wpart[i].astype(F32)
    gwbuf[rep] = chunk_sum
    v_in = []
    for d in (6, 2, 5, 7, 3, 1, 4):
        v_in.append(push(gwbuf.at[rep], gwbuf.at[rep], v_s.at[d], v_r.at[d], at(dr=d)))
    total = cstage[z].astype(F32)
    for d, copy in zip((7, 1, 6, 2, 5, 3, 4), reversed(b_in)):
        copy.wait_recv()
        total += cin[d].astype(F32)
    grad_feats[...] = total.astype(BF16)
    for copy in reversed(v_in):
        copy.wait_recv()
    grad_weight[...] = gwbuf[...].reshape(FEAT, FEAT)
    for copy in sends:
        copy.wait_send()


def per_device(
    node_feats, weight_matrix, tile_values, tile_rows, tile_cols, tile_count, labelled, upstream
):
    any_space = pl.BlockSpec(memory_space=pl.ANY)
    vmem = pl.BlockSpec(memory_space=pltpu.VMEM)
    smem = pl.BlockSpec(memory_space=pltpu.SMEM)
    dma = pltpu.SemaphoreType.DMA
    return pl.pallas_call(
        kernel,
        name="graph_layer",
        out_shape=(
            jax.ShapeDtypeStruct((ROWS, FEAT), BF16),
            jax.ShapeDtypeStruct((ROWS, FEAT), BF16),
            jax.ShapeDtypeStruct((FEAT, FEAT), F32),
        ),
        in_specs=[any_space, any_space, any_space, vmem, vmem, smem, vmem, any_space],
        out_specs=(vmem, vmem, vmem),
        scratch_shapes=[
            pltpu.VMEM((COLS, TILE, FEAT), BF16),
            pltpu.VMEM((SLOTS + 1, TILE, TILE), BF16),
            pltpu.VMEM((NZ, TEAM, NY * TILE), BF16),
            pltpu.VMEM((FEAT, FEAT), BF16),
            pltpu.VMEM((TEAM, FEAT), BF16),
            pltpu.VMEM((1, TILE), I32),
            pltpu.SMEM((1, TILE), I32),
            pltpu.VMEM((TEAM, FEAT), F32),
            pltpu.VMEM((NY, NZ, LAB, TILE), BF16),
            pltpu.VMEM((NY, NZ, LAB, TILE), BF16),
            pltpu.VMEM((NZ, TILE, TILE), BF16),
            pltpu.VMEM((NZ, ROWS, NC * TILE), BF16),
            pltpu.VMEM((NR, ROWS + LAB, FEAT), BF16),
            pltpu.VMEM((NR, ROWS + LAB, FEAT), BF16),
            pltpu.VMEM((NC * NY, LAB, FEAT + TILE), BF16),
            pltpu.VMEM((NZ, LAB, FEAT), BF16),
            pltpu.VMEM((NZ, ROWS, FEAT), BF16),
            pltpu.VMEM((NZ, ROWS, FEAT), BF16),
            pltpu.VMEM((NR, LAB, FEAT), F32),
            dma((5,)),
            dma((4,)), dma((4,)), dma((2, 5, 4)), dma((2, 5, 4)), dma((32,)), dma((32,)),
            dma((4,)), dma((4,)), dma((1,)), dma((1,)),
            dma((8,)), dma((8,)), dma((8,)), dma((8,)), dma((8,)), dma((8,)),
            dma((8,)), dma((8,)), dma((8,)), dma((8,)),
        ],
        compiler_params=pltpu.CompilerParams(
            collective_id=0, has_side_effects=True, vmem_limit_bytes=40 * 2**20
        ),
    )(
        node_feats, weight_matrix, tile_values, tile_rows.reshape(1, SLOTS), tile_cols.reshape(1, SLOTS),
        tile_count.reshape(1, 1), labelled, upstream,
    )


def solution(mesh):
    placed = (
        P(("loop", "rep"), None),
        P(),
        P(("loop", "rep"), None, None),
        P(("loop", "rep")),
        P(("loop", "rep")),
        P(("loop", "rep")),
        P("loop", None),
        P("loop", None),
    )
    return jax.shard_map(
        per_device,
        mesh=mesh,
        in_specs=placed,
        out_specs=(P(("loop", "rep"), None), P(("loop", "rep"), None), P()),
        check_vma=False,
    )
```

```python
import jax
import jax.numpy as jnp
from jax import lax
from jax.experimental import pallas as pl
from jax.experimental.pallas import tpu as pltpu
from jax.sharding import PartitionSpec as P

MESH = pl.DeviceIdType.MESH
NZ, NY, NC, NR = 8, 4, 2, 8
ROWS, FEAT, TILE, SLOTS = 64, 256, 128, 64
TEAM, LAB, RT = 512, 32, 4
REP_HALF = (ROWS + LAB) // 2
HALF = LAB // NC
COLS = NZ * NY
F32, BF16, I32 = jnp.float32, jnp.bfloat16, jnp.int32
CONTRACT_ROWS = (((0,), (0,)), ((), ()))
CONTRACT_LANES = (((1,), (1,)), ((), ()))


def iota(shape, dim):
    return lax.broadcasted_iota(I32, shape, dim)


def to_column(row):
    n = row.shape[1]
    square = jnp.broadcast_to(row, (n, n))
    return jnp.sum(jnp.where(iota((n, n), 0) == iota((n, n), 1), square, 0), axis=1, keepdims=True)


def kernel(
    feats, weight, values, trows_h, tcols_h, tcount_h, lab_h, upstream,
    layer_out, grad_feats, grad_weight,
    x3, tiles, dense, wv, upv, trows, tcols, lab, tcount, table_v, table_s, acc, asub, a4, at4, at8,
    stage, rep_in, relay_in, msg, wpart, part_v, cstage, cin, gwbuf, z_relay,
    local_sem, y_s, y_r, h_s, h_r, z_s, z_r, c_s, c_r, l_s, l_r, a_s, a_r, t_s, t_r,
    q_s, q_r, rep_s, rep_r, m_s, m_r, w_s, w_r, b_s, b_r, f_s, f_r, v_s, v_r,
):
    loop, rep = lax.axis_index("loop"), lax.axis_index("rep")
    z, yh, c = loop // 8, (loop // 2) % 4, loop % 2

    def at(dz=0, dy=0, dc=0, dr=0):
        nz, ny = lax.rem(z + dz + NZ, NZ), lax.rem(yh + dy + NY, NY)
        nc, nr = lax.rem(c + dc, NC), lax.rem(rep + dr, NR)
        return (nz * 8 + ny * 2 + nc, nr)

    sends = []

    def push(src, dst, ss, rs, to):
        copy = pltpu.make_async_remote_copy(
            src_ref=src, dst_ref=dst, send_sem=ss, recv_sem=rs, device_id=to, device_id_type=MESH
        )
        copy.start()
        sends.append(copy)
        return copy

    small = [
        pltpu.make_async_copy(trows_h, trows, local_sem.at[5]),
        pltpu.make_async_copy(tcols_h, tcols, local_sem.at[6]),
        pltpu.make_async_copy(tcount_h, tcount, local_sem.at[7]),
        pltpu.make_async_copy(lab_h, lab, local_sem.at[8]),
    ]
    for load in small:
        load.start()
    loads = [
        pltpu.make_async_copy(values, tiles.at[pl.ds(0, SLOTS)], local_sem.at[0]),
        pltpu.make_async_copy(feats, x3.at[z * NY + yh, pl.ds(c * ROWS, ROWS)], local_sem.at[1]),
        pltpu.make_async_copy(weight, wv, local_sem.at[2]),
        pltpu.make_async_copy(upstream, upv, local_sem.at[3]),
    ]

    peers = [at(dz=i) for i in (4, 3, 5, 2, 6, 1, 7)]
    peers += [at(dy=i) for i in (2, 1, 3)] + [at(dc=1)]
    peers += [at(dr=i) for i in (6, 2, 5, 7, 3, 1, 4)]
    barrier = pltpu.get_barrier_semaphore()
    for peer in peers:
        pl.semaphore_signal(barrier, inc=1, device_id=peer, device_id_type=MESH)
    for load in loads:
        load.start()
    pl.semaphore_wait(barrier, len(peers))

    step = 1 - 2 * c

    def z_at(k):
        return lax.rem(z + k + NZ, NZ)

    def chip_block(k, jj):
        return x3.at[z_at(k) * NY + lax.rem(yh - jj + NY, NY)]

    def half_block(jj):
        return chip_block(0, jj).at[pl.ds(c * ROWS, ROWS)]

    y_in, half_in, z_in, sib_in, last_in = {}, {}, {}, {}, []

    def send_ring(s, jj):
        block = chip_block(-step * (s - 1), jj)
        if s == 4:
            block = block.at[pl.ds(c * ROWS, ROWS)]
        z_in[s, jj] = push(block, block, z_s.at[s, jj], z_r.at[s, jj], at(dz=step))

    def ring(s, jj):
        z_in[s, jj].wait_recv()
        if s < 4:
            send_ring(s + 1, jj)

    def send_sib(s):
        block = x3.at[pl.ds(z_at(-step * s) * NY, NY)]
        sib_in[s] = push(block, block, c_s.at[s], c_r.at[s], at(dc=1))

    def from_y(jj):
        y_in[jj].wait_recv()
        half_in[jj] = push(half_block(jj), half_block(jj), h_s.at[jj], h_r.at[jj], at(dc=1))

    def from_sib(jj):
        half_in[jj].wait_recv()
        send_ring(1, jj)

    half_in[0] = push(feats, half_block(0), h_s.at[0], h_r.at[0], at(dc=1))
    for jj in (2, 1, 3):
        y_in[jj] = push(feats, half_block(0), y_s.at[jj], y_r.at[jj], at(dy=jj))

    loads[1].wait()
    from_sib(0)

    for load in small:
        load.wait()
    pos = to_column(trows[...] * COLS + tcols[...])
    live = iota((SLOTS, 1), 0) < tcount[0]
    hit = (pos == iota((SLOTS, TILE), 1)) & live
    table_v[...] = SLOTS + jnp.sum(jnp.where(hit, iota((SLOTS, TILE), 0) - SLOTS, 0), axis=0, keepdims=True)
    table_copy = pltpu.make_async_copy(table_v, table_s, local_sem.at[4])
    table_copy.start()

    lab_row = lab[...]
    lab_col = to_column(lab_row)
    twice = (lab_col == lab_row) & (iota((LAB, LAB), 1) < iota((LAB, LAB), 0))
    first = jnp.sum(jnp.where(twice, 1, 0), axis=1, keepdims=True) == 0
    pick = jnp.where((lab_col == iota((LAB, TEAM), 1)) & first, 1.0, 0.0).astype(BF16)

    tiles[SLOTS] = jnp.zeros((TILE, TILE), BF16)

    def densify(nz, carry):
        for j in range(NY):
            for rt in range(RT):
                slot = table_s[0, rt * COLS + nz * NY + j]
                dense[nz, rt * TILE:(rt + 1) * TILE, j * TILE:(j + 1) * TILE] = tiles[slot]
        rows = jnp.dot(pick, dense[nz], preferred_element_type=F32).astype(BF16)
        for j in range(NY):
            asub[j, nz] = rows[:, j * TILE:(j + 1) * TILE]
        return carry

    def add_block(k, fresh=False):
        nz = z_at(k)
        block = x3[pl.ds(nz * NY, NY)].reshape(NY * TILE, FEAT)
        term = jnp.dot(dense[nz], block, preferred_element_type=F32)
        if fresh:
            acc[...] = term
        else:
            acc[...] += term

    loads[0].wait()
    table_copy.wait()
    lax.fori_loop(0, 3, densify, 0)
    from_y(1)
    from_y(3)
    ring(1, 0)
    from_sib(1)
    from_sib(3)
    from_y(2)
    lax.fori_loop(3, 5, densify, 0)
    from_sib(2)
    ring(2, 0)
    lax.fori_loop(5, NZ, densify, 0)
    a_in = {}
    for jj in (2, 1, 3):
        a_in[jj] = push(asub.at[lax.rem(yh + jj, NY)], a4.at[yh], a_s.at[jj], a_r.at[jj], at(dy=jj))
    a4[yh] = asub[yh]
    ring(1, 1)
    ring(1, 3)
    ring(3, 0)
    ring(1, 2)
    send_sib(1)
    add_block(0, fresh=True)
    for jj in (1, 3, 2):
        ring(2, jj)
    send_sib(2)
    add_block(-step)
    sib_in[1].wait_recv()
    add_block(step)
    for jj in (1, 3, 2):
        ring(3, jj)
    send_sib(3)
    add_block(-2 * step)
    sib_in[2].wait_recv()
    add_block(2 * step)
    for jj in (0, 1, 3, 2):
        ring(4, jj)
        block = chip_block(4, jj).at[pl.ds(c * ROWS, ROWS)]
        last_in.append(push(block, block, l_s.at[jj], l_r.at[jj], at(dc=1)))
    add_block(-3 * step)
    sib_in[3].wait_recv()
    add_block(3 * step)
    for copy in last_in:
        copy.wait_recv()
    add_block(4)

    low = acc[...].astype(BF16)
    picked = jnp.dot(pick, low, preferred_element_type=F32).astype(BF16)
    for i in range(NR):
        stage[i, 0:ROWS] = low[i * ROWS:(i + 1) * ROWS]
        stage[i, ROWS:ROWS + LAB] = picked
    x, yl = rep % 4, rep // 4

    def target(dx, dyl):
        return lax.rem(yl + dyl, 2) * 4 + lax.rem(x + dx + 4, 4)

    halves = (pl.ds(0, REP_HALF), pl.ds(REP_HALF, REP_HALF))
    relay, rep_arrivals = {}, []
    for dyl in (1, 0):
        for side, dx in enumerate((1, -1)):
            relay[side, dyl] = push(
                stage.at[target(2, dyl), halves[side]], relay_in.at[side, dyl],
                q_s.at[side, dyl], q_r.at[side, dyl], (loop, target(dx, 0)),
            )

    def send_rep(dx, dyl, part, i):
        to = target(dx, dyl)
        rep_arrivals.append(push(
            stage.at[to, part], rep_in.at[dyl * 3 + dx + 1, part], rep_s.at[i], rep_r.at[i], (loop, to)
        ))

    send_rep(0, 1, pl.ds(0, ROWS + LAB), 0)
    for dyl in (1, 0):
        for side, dx in enumerate((1, -1)):
            send_rep(dx, dyl, halves[1 - side], 1 + dyl * 2 + side)
    for dyl in (1, 0):
        for side, dx in enumerate((1, -1)):
            relay[side, dyl].wait_recv()
            to, part = target(dx, dyl), halves[side]
            merged = stage[to, part].astype(F32) + relay_in[side, dyl].astype(F32)
            stage[to, part] = merged.astype(BF16)
            send_rep(dx, dyl, part, 5 + dyl * 2 + side)
    gather_sends = list(sends)
    for jj in range(1, NY):
        a_in[jj].wait_recv()
    for i in range(NZ):
        block = jnp.concatenate([a4[j, i] for j in range(NY)], axis=0)
        at4[i] = block.astype(F32).T.astype(BF16)
    t_in = push(
        at4.at[:, pl.ds((1 - c) * ROWS, ROWS)], at8.at[:, :, pl.ds(c * TILE, TILE)],
        t_s.at[0], t_r.at[0], at(dc=1),
    )
    at8[:, :, pl.ds(pl.multiple_of(c * TILE, TILE), TILE)] = at4[:, pl.ds(pl.multiple_of(c * ROWS, ROWS), ROWS)]
    for copy in gather_sends:
        copy.wait_send()
    loads[2].wait()
    loads[3].wait()
    w = wv[...]
    up_lab = jnp.dot(pick, upv[...], preferred_element_type=F32)
    total = stage[rep].astype(F32)
    for copy in rep_arrivals:
        copy.wait_recv()
    for i in (0, 2, 3, 4, 5):
        total += rep_in[i].astype(F32)
    agg = total.astype(BF16)
    pre = jnp.dot(agg, w, preferred_element_type=F32)
    gate = jax.nn.sigmoid(pre)
    layer_out[...] = (pre * gate)[0:ROWS].astype(BF16)
    pre_l, gate_l = pre[ROWS:], gate[ROWS:]
    slope = gate_l * (1.0 + pre_l * (1.0 - gate_l))
    mine = c * NY + yh
    msg[mine, :, 0:FEAT] = (up_lab * slope).astype(BF16)
    chunk = (iota((FEAT, TILE), 0) == rep * LAB + iota((FEAT, TILE), 1)) & (iota((FEAT, TILE), 1) < LAB)
    msg[mine, :, FEAT:] = jnp.dot(
        agg[ROWS:], jnp.where(chunk, 1.0, 0.0).astype(BF16), preferred_element_type=F32
    ).astype(BF16)
    m_in, m_sib = {}, []
    for dy in (2, 1, 3):
        m_in[dy] = push(msg.at[mine], msg.at[mine], m_s.at[dy], m_r.at[dy], at(dy=dy))

    def pass_msg(dy):
        slot = msg.at[c * NY + lax.rem(yh - dy + NY, NY)]
        m_sib.append(push(slot, slot, m_s.at[4 + dy], m_r.at[4 + dy], at(dc=1)))

    pass_msg(0)
    t_in.wait_recv()
    for dy in (1, 3, 2):
        m_in[dy].wait_recv()
        pass_msg(dy)
    for copy in m_sib:
        copy.wait_recv()

    grad_pre = msg[:, :, 0:FEAT].reshape(NC * NY * LAB, FEAT)
    agg_chunk = msg[:, :, FEAT:].reshape(NC * NY * LAB, TILE)
    part = lax.dot_general(agg_chunk, grad_pre, CONTRACT_ROWS, preferred_element_type=F32)
    part_v[...] = part[0:LAB]
    wpart[z] = part_v[pl.ds(pl.multiple_of(c * HALF, HALF), HALF)].astype(BF16)
    w_in, b_in = [], []
    for d in (4, 3, 5, 2, 6, 1, 7):
        w_in.append(push(wpart.at[z], wpart.at[z], w_s.at[d], w_r.at[d], at(dz=d)))
    grad_agg = lax.dot_general(grad_pre, w, CONTRACT_LANES, preferred_element_type=F32).astype(BF16)
    term = jnp.dot(at8[...].reshape(NZ * ROWS, NC * NY * LAB), grad_agg, preferred_element_type=F32)
    cstage[...] = term.astype(BF16).reshape(NZ, ROWS, FEAT)
    top, bottom = pl.ds(0, ROWS // 2), pl.ds(ROWS // 2, ROWS // 2)
    far = [
        push(cstage.at[z_at(4), top], z_relay.at[0], f_s.at[0], f_r.at[0], at(dz=3)),
        push(cstage.at[z_at(4), bottom], z_relay.at[1], f_s.at[1], f_r.at[1], at(dz=-3)),
    ]
    for d in (3, -3, 2, -2):
        b_in.append(push(cstage.at[z_at(d)], cin.at[d % NZ], b_s.at[d % NZ], b_r.at[d % NZ], at(dz=d)))
    b_in.append(push(cstage.at[z_at(1), bottom], cin.at[1, bottom], b_s.at[1], b_r.at[1], at(dz=1)))
    b_in.append(push(cstage.at[z_at(-1), top], cin.at[7, top], b_s.at[7], b_r.at[7], at(dz=-1)))
    for copy in reversed(w_in):
        copy.wait_recv()
    chunk_sum = wpart[0].astype(F32)
    for i in range(1, NZ):
        chunk_sum += wpart[i].astype(F32)
    gwbuf[rep, c] = chunk_sum.astype(BF16)
    v_in = []
    for d in (6, 2, 5, 7, 3, 1, 4):
        v_in.append(push(gwbuf.at[rep, c], gwbuf.at[rep, c], v_s.at[d], v_r.at[d], at(dr=d)))
    for i, (d, part) in enumerate(((1, top), (-1, bottom))):
        far[i].wait_recv()
        merged = cstage[z_at(d), part].astype(F32) + z_relay[i].astype(F32)
        cstage[z_at(d), part] = merged.astype(BF16)
        b_in.append(push(cstage.at[z_at(d), part], cin.at[d % NZ, part], f_s.at[2 + i], f_r.at[2 + i], at(dz=d)))
    for copy in reversed(v_in):
        copy.wait_recv()
    v_sib = push(gwbuf.at[:, c], gwbuf.at[:, c], v_s.at[0], v_r.at[0], at(dc=1))
    total = cstage[z].astype(F32)
    for copy in b_in:
        copy.wait_recv()
    for d in (1, 2, 3, 5, 6, 7):
        total += cin[d].astype(F32)
    grad_feats[...] = total.astype(BF16)
    for copy in sends[len(gather_sends):]:
        copy.wait_send()
    v_sib.wait_recv()
    grad_weight[...] = gwbuf[...].astype(F32).reshape(FEAT, FEAT)


def write_out(layer_in, feats_in, weight_in, layer_out, grad_feats, grad_weight):
    layer_out[...] = layer_in[...]
    grad_feats[...] = feats_in[...]
    grad_weight[...] = weight_in[...]


def per_device(
    node_feats, weight_matrix, tile_values, tile_rows, tile_cols, tile_count, labelled, upstream
):
    hbm = pl.BlockSpec(memory_space=pl.ANY)
    vmem = pl.BlockSpec(memory_space=pltpu.VMEM)
    dma = pltpu.SemaphoreType.DMA
    shapes = (
        jax.ShapeDtypeStruct((ROWS, FEAT), BF16),
        jax.ShapeDtypeStruct((ROWS, FEAT), BF16),
        jax.ShapeDtypeStruct((FEAT, FEAT), F32),
    )
    results = pl.pallas_call(
        kernel,
        name="graph_layer",
        out_shape=shapes,
        in_specs=[hbm] * 8,
        out_specs=(vmem, vmem, vmem),
        scratch_shapes=[
            pltpu.VMEM((COLS, TILE, FEAT), BF16),
            pltpu.VMEM((SLOTS + 1, TILE, TILE), BF16),
            pltpu.VMEM((NZ, TEAM, NY * TILE), BF16),
            pltpu.VMEM((FEAT, FEAT), BF16),
            pltpu.VMEM((TEAM, FEAT), BF16),
            pltpu.VMEM((1, SLOTS), I32),
            pltpu.VMEM((1, SLOTS), I32),
            pltpu.VMEM((1, LAB), I32),
            pltpu.SMEM((1,), I32),
            pltpu.VMEM((1, TILE), I32),
            pltpu.SMEM((1, TILE), I32),
            pltpu.VMEM((TEAM, FEAT), F32),
            pltpu.VMEM((NY, NZ, LAB, TILE), BF16),
            pltpu.VMEM((NY, NZ, LAB, TILE), BF16),
            pltpu.VMEM((NZ, TILE, TILE), BF16),
            pltpu.VMEM((NZ, ROWS, NC * TILE), BF16),
            pltpu.VMEM((NR, ROWS + LAB, FEAT), BF16),
            pltpu.VMEM((6, ROWS + LAB, FEAT), BF16),
            pltpu.VMEM((2, 2, REP_HALF, FEAT), BF16),
            pltpu.VMEM((NC * NY, LAB, FEAT + TILE), BF16),
            pltpu.VMEM((NZ, HALF, FEAT), BF16),
            pltpu.VMEM((LAB, FEAT), F32),
            pltpu.VMEM((NZ, ROWS, FEAT), BF16),
            pltpu.VMEM((NZ, ROWS, FEAT), BF16),
            pltpu.VMEM((NR, NC, HALF, FEAT), BF16),
            pltpu.VMEM((2, ROWS // 2, FEAT), BF16),
            dma((9,)),
            dma((4,)), dma((4,)), dma((4,)), dma((4,)), dma((5, 4)), dma((5, 4)), dma((4,)), dma((4,)), dma((4,)), dma((4,)),
            dma((4,)), dma((4,)), dma((1,)), dma((1,)),
            dma((2, 2)), dma((2, 2)), dma((9,)), dma((9,)), dma((8,)), dma((8,)), dma((8,)), dma((8,)),
            dma((8,)), dma((8,)), dma((4,)), dma((4,)), dma((8,)), dma((8,)),
        ],
        compiler_params=pltpu.CompilerParams(
            collective_id=0, has_side_effects=True, vmem_limit_bytes=60 * 2**20
        ),
    )(
        node_feats, weight_matrix, tile_values, tile_rows.reshape(1, SLOTS), tile_cols.reshape(1, SLOTS),
        tile_count, labelled, upstream,
    )
    return pl.pallas_call(
        write_out,
        name="write_out",
        out_shape=shapes,
        in_specs=[vmem] * 3,
        out_specs=(vmem,) * 3,
        compiler_params=pltpu.CompilerParams(vmem_limit_bytes=60 * 2**20),
    )(*results)


def solution(mesh):
    placed = (
        P(("loop", "rep"), None),
        P(),
        P(("loop", "rep"), None, None),
        P(("loop", "rep")),
        P(("loop", "rep")),
        P(("loop", "rep")),
        P("loop", None),
        P("loop", None),
    )
    return jax.shard_map(
        per_device,
        mesh=mesh,
        in_specs=placed,
        out_specs=(P(("loop", "rep"), None), P(("loop", "rep"), None), P()),
        check_vma=False,
    )
```

```python
import jax
import jax.numpy as jnp
from jax import lax
from jax.experimental import pallas as pl
from jax.experimental.pallas import tpu as pltpu
from jax.sharding import PartitionSpec as P

MESH = pl.DeviceIdType.MESH
NZ, NY, NC, NR = 8, 4, 2, 8
ROWS, FEAT, TILE, SLOTS = 64, 256, 128, 64
TEAM, LAB, RT = 512, 32, 4
REP_HALF = ROWS + LAB
HALF = LAB // NC
COLS = NZ * NY
F32, BF16, I32 = jnp.float32, jnp.bfloat16, jnp.int32
CONTRACT_ROWS = (((0,), (0,)), ((), ()))
CONTRACT_LANES = (((1,), (1,)), ((), ()))


def iota(shape, dim):
    return lax.broadcasted_iota(I32, shape, dim)


def to_column(row):
    n = row.shape[1]
    square = jnp.broadcast_to(row, (n, n))
    return jnp.sum(jnp.where(iota((n, n), 0) == iota((n, n), 1), square, 0), axis=1, keepdims=True)


def kernel(
    feats, weight, values, trows_h, tcols_h, tcount_h, lab_h, upstream,
    layer_out, grad_feats, grad_weight,
    x3, tiles, tiles_sib, dense, wv, upv, trows, tcols, lab, tcount, info, info_sib, table_s, acc, asub, a4, at4, at8,
    stage, rep_in, relay_in, msg, chunk, wpart, ypart, part_v, cstage, cin, gwbuf, z_relay,
    local_sem, y_s, y_r, h_s, h_r, z_s, z_r, a_s, a_r, t_s, t_r,
    q_s, q_r, rep_s, rep_r, m_s, m_r, w_s, w_r, u_s, u_r, b_s, b_r, f_s, f_r, v_s, v_r,
):
    loop, rep = lax.axis_index("loop"), lax.axis_index("rep")
    z, yh, c = loop // 8, (loop // 2) % 4, loop % 2

    def at(dz=0, dy=0, dc=0, dr=0):
        nz, ny = lax.rem(z + dz + NZ, NZ), lax.rem(yh + dy + NY, NY)
        nc, nr = lax.rem(c + dc, NC), lax.rem(rep + dr, NR)
        return (nz * 8 + ny * 2 + nc, nr)

    sends = []

    def push(src, dst, ss, rs, to):
        copy = pltpu.make_async_remote_copy(
            src_ref=src, dst_ref=dst, send_sem=ss, recv_sem=rs, device_id=to, device_id_type=MESH
        )
        copy.start()
        sends.append(copy)
        return copy

    small = [
        pltpu.make_async_copy(trows_h, trows, local_sem.at[5]),
        pltpu.make_async_copy(tcols_h, tcols, local_sem.at[6]),
        pltpu.make_async_copy(tcount_h, tcount, local_sem.at[7]),
        pltpu.make_async_copy(lab_h, lab, local_sem.at[8]),
    ]
    for load in small:
        load.start()
    lanes = pl.ds(pl.multiple_of(c * TILE, TILE), TILE)
    other_lanes = pl.ds(pl.multiple_of((1 - c) * TILE, TILE), TILE)
    own_rows = pl.ds(pl.multiple_of(c * ROWS, ROWS), ROWS)
    own_half = x3.at[z * NY + yh, own_rows]
    loads = [
        pltpu.make_async_copy(values, tiles.at[pl.ds(0, SLOTS)], local_sem.at[0]),
        pltpu.make_async_copy(feats.at[:, lanes], own_half, local_sem.at[1]),
        pltpu.make_async_copy(weight, wv, local_sem.at[2]),
        pltpu.make_async_copy(upstream, upv, local_sem.at[3]),
    ]

    peers = [at(dz=i) for i in (4, 3, 5, 2, 6, 1, 7)]
    peers += [at(dy=i, dc=k) for i in (2, 1, 3) for k in range(NC)] + [at(dc=1)]
    peers += [at(dr=i) for i in (6, 2, 5, 7, 3, 1, 4)]
    x, yl = rep % 4, rep // 4

    def target(dx, dyl):
        return lax.rem(yl + dyl, 2) * 4 + lax.rem(x + dx + 4, 4)

    near = ((1, 1), (-1, 1), (0, 1), (1, 0), (-1, 0))
    peers += [(at(dc=1)[0], target(dx, dyl)) for dx, dyl in near]
    barrier = pltpu.get_barrier_semaphore()
    for peer in peers:
        pl.semaphore_signal(barrier, inc=1, device_id=peer, device_id_type=MESH)
    for load in loads:
        load.start()
    pl.semaphore_wait(barrier, len(peers))

    def z_at(k):
        return lax.rem(z + k + NZ, NZ)

    def chip_block(k, jj):
        return x3.at[z_at(k) * NY + lax.rem(yh - jj + NY, NY)]

    y_in, up_in, down_in = {}, {}, {}

    def send_up(s, jj):
        block = chip_block(1 - s, jj)
        if s == 4:
            block = block.at[pl.ds(0, ROWS)]
        up_in[s, jj] = push(block, block, z_s.at[0, s, jj], z_r.at[0, s, jj], at(dz=1))

    def send_down(s, jj):
        block = chip_block(s - 1, jj)
        if s == 4:
            block = block.at[pl.ds(ROWS, ROWS)]
        down_in[s, jj] = push(block, block, z_s.at[1, s, jj], z_r.at[1, s, jj], at(dz=-1))

    def send_ring(s, jj):
        send_up(s, jj)
        send_down(s, jj)

    def ring(s, jj):
        up_in[s, jj].wait_recv()
        if s < 4:
            send_up(s + 1, jj)
        down_in[s, jj].wait_recv()
        if s < 4:
            send_down(s + 1, jj)

    def from_y(jj):
        y_in[jj, 0].wait_recv()
        y_in[jj, 1].wait_recv()
        send_ring(1, jj)

    sib_own = push(feats.at[:, other_lanes], own_half, h_s.at[0], h_r.at[0], at(dc=1))
    for jj in (2, 1, 3):
        y_in[jj, 0] = push(feats.at[:, lanes], own_half, y_s.at[jj, 0], y_r.at[jj, 0], at(dy=jj))
        y_in[jj, 1] = push(feats.at[:, other_lanes], own_half, y_s.at[jj, 1], y_r.at[jj, 1], at(dy=jj, dc=1))
    tiles_in = push(values, tiles_sib.at[pl.ds(0, SLOTS)], h_s.at[1], h_r.at[1], at(dc=1))

    for load in small:
        load.wait()
    pos = to_column(trows[...] * COLS + tcols[...])
    live = iota((SLOTS, 1), 0) < tcount[0]
    hit = (pos == iota((SLOTS, TILE), 1)) & live
    info[...] = jnp.zeros_like(info)
    info[0:1] = SLOTS + jnp.sum(jnp.where(hit, iota((SLOTS, TILE), 0) - SLOTS, 0), axis=0, keepdims=True)
    info[1:2, 0:LAB] = lab[...]
    info_in = push(info, info_sib, h_s.at[2], h_r.at[2], at(dc=1))
    table_copy = pltpu.make_async_copy(info, table_s.at[0], local_sem.at[4])
    table_copy.start()

    loads[1].wait()
    sib_own.wait_recv()
    send_ring(1, 0)

    def picker(lab_row):
        lab_col = to_column(lab_row)
        twice = (lab_col == lab_row) & (iota((LAB, LAB), 1) < iota((LAB, LAB), 0))
        first = jnp.sum(jnp.where(twice, 1, 0), axis=1, keepdims=True) == 0
        return jnp.where((lab_col == iota((LAB, TEAM), 1)) & first, 1.0, 0.0).astype(BF16)

    pick = picker(lab[...])
    tiles[SLOTS] = jnp.zeros((TILE, TILE), BF16)
    tiles_sib[SLOTS] = jnp.zeros((TILE, TILE), BF16)

    def densify(team, held, nz):
        for j in range(NY):
            for rt in range(RT):
                slot = table_s[team, 0, rt * COLS + nz * NY + j]
                dense[team, nz, rt * TILE:(rt + 1) * TILE, j * TILE:(j + 1) * TILE] = held[slot]

    def densify_own(nz, carry):
        densify(0, tiles, nz)
        rows = jnp.dot(pick, dense[0, nz], preferred_element_type=F32).astype(BF16)
        for j in range(NY):
            asub[j, nz] = rows[:, j * TILE:(j + 1) * TILE]
        return carry

    def densify_sib(nz, carry):
        densify(1, tiles_sib, nz)
        return carry

    def add_block(k, fresh=False):
        nz = z_at(k)
        block = x3[pl.ds(nz * NY, NY)].reshape(NY * TILE, TILE)
        for team in range(NC):
            term = jnp.dot(dense[team, nz], block, preferred_element_type=F32)
            if fresh:
                acc[team] = term
            else:
                acc[team] += term

    loads[0].wait()
    table_copy.wait()
    lax.fori_loop(0, 4, densify_own, 0)
    from_y(1)
    from_y(3)
    ring(1, 0)
    from_y(2)
    lax.fori_loop(4, NZ, densify_own, 0)
    a_in = {}
    for jj in (2, 1, 3):
        a_in[jj] = push(asub.at[lax.rem(yh + jj, NY)], a4.at[yh], a_s.at[jj], a_r.at[jj], at(dy=jj))
    ring(1, 1)
    ring(1, 3)
    ring(2, 0)
    ring(1, 2)
    a4[yh] = asub[yh]
    info_in.wait_recv()
    sib_table = pltpu.make_async_copy(info_sib, table_s.at[1], local_sem.at[9])
    sib_table.start()
    pick_sib = picker(info_sib[1:2, 0:LAB])
    ring(2, 1)
    ring(2, 3)
    ring(3, 0)
    ring(2, 2)
    sib_table.wait()
    tiles_in.wait_recv()
    lax.fori_loop(0, NZ, densify_sib, 0)
    ring(3, 1)
    ring(3, 3)
    ring(3, 2)
    add_block(0, fresh=True)
    add_block(1)
    add_block(-1)
    add_block(2)
    add_block(-2)
    add_block(3)
    add_block(-3)
    for jj in (0, 1, 3, 2):
        ring(4, jj)
    add_block(4)

    for team, rows in enumerate((pick, pick_sib)):
        low = acc[team].astype(BF16)
        picked = jnp.dot(rows, low, preferred_element_type=F32).astype(BF16)
        base = team * REP_HALF
        for i in range(NR):
            stage[i, base:base + ROWS] = low[i * ROWS:(i + 1) * ROWS]
            stage[i, base + ROWS:base + REP_HALF] = picked
    halves = (pl.ds(0, REP_HALF), pl.ds(REP_HALF, REP_HALF))
    relay, rep_arrivals = {}, []
    for dyl in (1, 0):
        for side, dx in enumerate((1, -1)):
            relay[side, dyl] = push(
                stage.at[target(2, dyl), halves[side]], relay_in.at[side, dyl],
                q_s.at[side, dyl], q_r.at[side, dyl], (loop, target(dx, 0)),
            )

    def send_rep(dx, dyl, side):
        to, slot = target(dx, dyl), dyl * 3 + dx + 1
        rep_arrivals.append(push(
            stage.at[to, halves[side]], rep_in.at[slot, :, lanes],
            rep_s.at[slot, side], rep_r.at[slot, side], (at(dc=side)[0], to),
        ))

    send_rep(0, 1, 0)
    send_rep(0, 1, 1)
    for dyl in (1, 0):
        for side, dx in enumerate((1, -1)):
            send_rep(dx, dyl, 1 - side)
    send_rep(0, 0, 1)
    rep_in[1, :, lanes] = stage[rep, 0:REP_HALF]
    for dyl in (1, 0):
        for side, dx in enumerate((1, -1)):
            relay[side, dyl].wait_recv()
            to, part = target(dx, dyl), halves[side]
            merged = stage[to, part].astype(F32) + relay_in[side, dyl].astype(F32)
            stage[to, part] = merged.astype(BF16)
            send_rep(dx, dyl, side)
    gather_sends = list(sends)
    for jj in range(1, NY):
        a_in[jj].wait_recv()
    for i in range(NZ):
        block = jnp.concatenate([a4[j, i] for j in range(NY)], axis=0)
        at4[i] = block.astype(F32).T.astype(BF16)
    t_in = push(
        at4.at[:, pl.ds((1 - c) * ROWS, ROWS)], at8.at[:, :, pl.ds(c * TILE, TILE)],
        t_s.at[0], t_r.at[0], at(dc=1),
    )
    at8[:, :, pl.ds(pl.multiple_of(c * TILE, TILE), TILE)] = at4[:, pl.ds(pl.multiple_of(c * ROWS, ROWS), ROWS)]
    for copy in gather_sends:
        copy.wait_send()
    loads[2].wait()
    loads[3].wait()
    w = wv[...]
    up_lab = jnp.dot(pick, upv[...], preferred_element_type=F32)
    for copy in rep_arrivals:
        copy.wait_recv()
    total = rep_in[0].astype(F32)
    for i in range(1, 6):
        total += rep_in[i].astype(F32)
    agg = total.astype(BF16)
    pre = jnp.dot(agg, w, preferred_element_type=F32)
    gate = jax.nn.sigmoid(pre)
    layer_out[...] = (pre * gate)[0:ROWS].astype(BF16)
    pre_l, gate_l = pre[ROWS:], gate[ROWS:]
    slope = gate_l * (1.0 + pre_l * (1.0 - gate_l))
    mine = c * NY + yh
    msg[mine] = (up_lab * slope).astype(BF16)
    m_in, m_sib = {}, []
    for dy in (2, 1, 3):
        m_in[dy] = push(msg.at[mine], msg.at[mine], m_s.at[dy], m_r.at[dy], at(dy=dy))

    def pass_msg(dy):
        slot = msg.at[c * NY + lax.rem(yh - dy + NY, NY)]
        m_sib.append(push(slot, slot, m_s.at[4 + dy], m_r.at[4 + dy], at(dc=1)))

    pass_msg(0)
    chosen = (iota((FEAT, TILE), 0) == rep * LAB + iota((FEAT, TILE), 1)) & (iota((FEAT, TILE), 1) < LAB)
    chunk[c] = jnp.dot(agg[ROWS:], jnp.where(chosen, 1.0, 0.0).astype(BF16), preferred_element_type=F32).astype(BF16)
    chunk_in = push(chunk.at[c], chunk.at[c], m_s.at[0], m_r.at[0], at(dc=1))
    m_sib[0].wait_recv()
    chunk_in.wait_recv()
    part = lax.dot_general(
        chunk[...].reshape(NC * LAB, TILE), jnp.concatenate([msg[yh], msg[NY + yh]], axis=0),
        CONTRACT_ROWS, preferred_element_type=F32,
    )
    part_v[...] = part[0:LAB]
    wpart[z] = part_v[pl.ds(pl.multiple_of(c * HALF, HALF), HALF)].astype(BF16)
    w_in, b_in = [], []
    for d in (4, 3, 5, 2, 6, 1, 7):
        w_in.append(push(wpart.at[z], wpart.at[z], w_s.at[d], w_r.at[d], at(dz=d)))
    t_in.wait_recv()
    for dy in (1, 3, 2):
        m_in[dy].wait_recv()
        pass_msg(dy)
    for copy in m_sib[1:]:
        copy.wait_recv()

    grad_pre = msg[...].reshape(NC * NY * LAB, FEAT)
    grad_agg = lax.dot_general(grad_pre, w, CONTRACT_LANES, preferred_element_type=F32).astype(BF16)
    term = jnp.dot(at8[...].reshape(NZ * ROWS, NC * NY * LAB), grad_agg, preferred_element_type=F32)
    cstage[...] = term.astype(BF16).reshape(NZ, ROWS, FEAT)
    top, bottom = pl.ds(0, ROWS // 2), pl.ds(ROWS // 2, ROWS // 2)
    far = [
        push(cstage.at[z_at(4), top], z_relay.at[0], f_s.at[0], f_r.at[0], at(dz=3)),
        push(cstage.at[z_at(4), bottom], z_relay.at[1], f_s.at[1], f_r.at[1], at(dz=-3)),
    ]
    for d in (3, -3, 2, -2):
        b_in.append(push(cstage.at[z_at(d)], cin.at[d % NZ], b_s.at[d % NZ], b_r.at[d % NZ], at(dz=d)))
    b_in.append(push(cstage.at[z_at(1), bottom], cin.at[1, bottom], b_s.at[1], b_r.at[1], at(dz=1)))
    b_in.append(push(cstage.at[z_at(-1), top], cin.at[7, top], b_s.at[7], b_r.at[7], at(dz=-1)))
    for copy in reversed(w_in):
        copy.wait_recv()
    chunk_sum = wpart[0].astype(F32)
    for i in range(1, NZ):
        chunk_sum += wpart[i].astype(F32)
    ypart[yh, c] = chunk_sum.astype(BF16)
    u_in = []
    for dy, dc in ((2, 1), (2, 0), (1, 1), (3, 1), (1, 0), (3, 0), (0, 1)):
        u_in.append(push(
            ypart.at[yh, c], ypart.at[yh, c], u_s.at[dc * NY + dy], u_r.at[dc * NY + dy], at(dy=dy, dc=dc)
        ))
    for copy in u_in:
        copy.wait_recv()
    chunk_sum = ypart[0].astype(F32)
    for i in range(1, NY):
        chunk_sum += ypart[i].astype(F32)
    gwbuf[rep] = chunk_sum.astype(BF16)
    v_in = []
    for d in (6, 2, 5, 7, 3, 1, 4):
        v_in.append(push(gwbuf.at[rep], gwbuf.at[rep], v_s.at[d], v_r.at[d], at(dr=d)))
    for i, (d, part) in enumerate(((1, top), (-1, bottom))):
        far[i].wait_recv()
        merged = cstage[z_at(d), part].astype(F32) + z_relay[i].astype(F32)
        cstage[z_at(d), part] = merged.astype(BF16)
        b_in.append(push(cstage.at[z_at(d), part], cin.at[d % NZ, part], f_s.at[2 + i], f_r.at[2 + i], at(dz=d)))
    total = cstage[z].astype(F32)
    for copy in b_in:
        copy.wait_recv()
    for d in (1, 2, 3, 5, 6, 7):
        total += cin[d].astype(F32)
    grad_feats[...] = total.astype(BF16)
    for copy in sends[len(gather_sends):]:
        copy.wait_send()
    for copy in reversed(v_in):
        copy.wait_recv()
    grad_weight[...] = gwbuf[...].astype(F32).reshape(FEAT, FEAT)


def write_out(layer_in, feats_in, weight_in, layer_out, grad_feats, grad_weight):
    layer_out[...] = layer_in[...]
    grad_feats[...] = feats_in[...]
    grad_weight[...] = weight_in[...]


def per_device(
    node_feats, weight_matrix, tile_values, tile_rows, tile_cols, tile_count, labelled, upstream
):
    hbm = pl.BlockSpec(memory_space=pl.ANY)
    vmem = pl.BlockSpec(memory_space=pltpu.VMEM)
    dma = pltpu.SemaphoreType.DMA
    shapes = (
        jax.ShapeDtypeStruct((ROWS, FEAT), BF16),
        jax.ShapeDtypeStruct((ROWS, FEAT), BF16),
        jax.ShapeDtypeStruct((FEAT, FEAT), F32),
    )
    results = pl.pallas_call(
        kernel,
        name="graph_layer",
        out_shape=shapes,
        in_specs=[hbm] * 8,
        out_specs=(vmem, vmem, vmem),
        scratch_shapes=[
            pltpu.VMEM((COLS, TILE, TILE), BF16),
            pltpu.VMEM((SLOTS + 1, TILE, TILE), BF16),
            pltpu.VMEM((SLOTS + 1, TILE, TILE), BF16),
            pltpu.VMEM((NC, NZ, TEAM, NY * TILE), BF16),
            pltpu.VMEM((FEAT, FEAT), BF16),
            pltpu.VMEM((TEAM, FEAT), BF16),
            pltpu.VMEM((1, SLOTS), I32),
            pltpu.VMEM((1, SLOTS), I32),
            pltpu.VMEM((1, LAB), I32),
            pltpu.SMEM((1,), I32),
            pltpu.VMEM((8, TILE), I32),
            pltpu.VMEM((8, TILE), I32),
            pltpu.SMEM((NC, 8, TILE), I32),
            pltpu.VMEM((NC, TEAM, TILE), F32),
            pltpu.VMEM((NY, NZ, LAB, TILE), BF16),
            pltpu.VMEM((NY, NZ, LAB, TILE), BF16),
            pltpu.VMEM((NZ, TILE, TILE), BF16),
            pltpu.VMEM((NZ, ROWS, NC * TILE), BF16),
            pltpu.VMEM((NR, NC * REP_HALF, TILE), BF16),
            pltpu.VMEM((6, REP_HALF, FEAT), BF16),
            pltpu.VMEM((2, 2, REP_HALF, TILE), BF16),
            pltpu.VMEM((NC * NY, LAB, FEAT), BF16),
            pltpu.VMEM((NC, LAB, TILE), BF16),
            pltpu.VMEM((NZ, HALF, FEAT), BF16),
            pltpu.VMEM((NY, NC, HALF, FEAT), BF16),
            pltpu.VMEM((LAB, FEAT), F32),
            pltpu.VMEM((NZ, ROWS, FEAT), BF16),
            pltpu.VMEM((NZ, ROWS, FEAT), BF16),
            pltpu.VMEM((NR, NC, HALF, FEAT), BF16),
            pltpu.VMEM((2, ROWS // 2, FEAT), BF16),
            dma((10,)),
            dma((4, 2)), dma((4, 2)), dma((4,)), dma((4,)), dma((2, 5, 4)), dma((2, 5, 4)),
            dma((4,)), dma((4,)), dma((1,)), dma((1,)),
            dma((2, 2)), dma((2, 2)), dma((6, 2)), dma((6, 2)), dma((8,)), dma((8,)), dma((8,)), dma((8,)), dma((8,)), dma((8,)),
            dma((8,)), dma((8,)), dma((4,)), dma((4,)), dma((8,)), dma((8,)),
        ],
        compiler_params=pltpu.CompilerParams(
            collective_id=0, has_side_effects=True, vmem_limit_bytes=60 * 2**20
        ),
    )(
        node_feats, weight_matrix, tile_values, tile_rows.reshape(1, SLOTS), tile_cols.reshape(1, SLOTS),
        tile_count, labelled, upstream,
    )
    return pl.pallas_call(
        write_out,
        name="write_out",
        out_shape=shapes,
        in_specs=[vmem] * 3,
        out_specs=(vmem,) * 3,
        compiler_params=pltpu.CompilerParams(vmem_limit_bytes=60 * 2**20),
    )(*results)


def solution(mesh):
    placed = (
        P(("loop", "rep"), None),
        P(),
        P(("loop", "rep"), None, None),
        P(("loop", "rep")),
        P(("loop", "rep")),
        P(("loop", "rep")),
        P("loop", None),
        P("loop", None),
    )
    return jax.shard_map(
        per_device,
        mesh=mesh,
        in_specs=placed,
        out_specs=(P(("loop", "rep"), None), P(("loop", "rep"), None), P()),
        check_vma=False,
    )
```

```python
import jax
import jax.numpy as jnp
from jax import lax
from jax.experimental import pallas as pl
from jax.experimental.pallas import tpu as pltpu
from jax.sharding import PartitionSpec as P

MESH = pl.DeviceIdType.MESH
NZ, NY, NC, NR = 8, 4, 2, 8
ROWS, FEAT, TILE, SLOTS = 64, 256, 128, 64
TEAM, LAB, RT = 512, 32, 4
REP_HALF = ROWS + LAB
HALF = LAB // NC
COLS = NZ * NY
F32, BF16, I32 = jnp.float32, jnp.bfloat16, jnp.int32
CONTRACT_ROWS = (((0,), (0,)), ((), ()))
CONTRACT_LANES = (((1,), (1,)), ((), ()))


def iota(shape, dim):
    return lax.broadcasted_iota(I32, shape, dim)


def to_column(row):
    n = row.shape[1]
    square = jnp.broadcast_to(row, (n, n))
    return jnp.sum(jnp.where(iota((n, n), 0) == iota((n, n), 1), square, 0), axis=1, keepdims=True)


def kernel(
    feats, weight, values, trows_h, tcols_h, tcount_h, lab_h, upstream,
    layer_out, grad_feats, grad_weight,
    x3, tiles, tiles_sib, dense, wv, upv, trows, tcols, lab, tcount, info, info_sib, table_s, acc, asub, a4, at4, at8,
    stage, rep_in, total_v, relay_in, msg, chunk, wpart, ypart, part_v, cstage, cin, gwbuf, z_relay,
    local_sem, y_s, y_r, h_s, h_r, z_s, z_r, a_s, a_r, t_s, t_r,
    q_s, q_r, rep_s, rep_r, m_s, m_r, w_s, w_r, u_s, u_r, b_s, b_r, f_s, f_r, v_s, v_r,
):
    loop, rep = lax.axis_index("loop"), lax.axis_index("rep")
    z, yh, c = loop // 8, (loop // 2) % 4, loop % 2

    def at(dz=0, dy=0, dc=0, dr=0):
        nz, ny = lax.rem(z + dz + NZ, NZ), lax.rem(yh + dy + NY, NY)
        nc, nr = lax.rem(c + dc, NC), lax.rem(rep + dr, NR)
        return (nz * 8 + ny * 2 + nc, nr)

    sends = []

    def push(src, dst, ss, rs, to):
        copy = pltpu.make_async_remote_copy(
            src_ref=src, dst_ref=dst, send_sem=ss, recv_sem=rs, device_id=to, device_id_type=MESH
        )
        copy.start()
        sends.append(copy)
        return copy

    small = [
        pltpu.make_async_copy(trows_h, trows, local_sem.at[5]),
        pltpu.make_async_copy(tcols_h, tcols, local_sem.at[6]),
        pltpu.make_async_copy(tcount_h, tcount, local_sem.at[7]),
        pltpu.make_async_copy(lab_h, lab, local_sem.at[8]),
    ]
    for load in small:
        load.start()
    lanes = pl.ds(pl.multiple_of(c * TILE, TILE), TILE)
    other_lanes = pl.ds(pl.multiple_of((1 - c) * TILE, TILE), TILE)
    own_rows = pl.ds(pl.multiple_of(c * ROWS, ROWS), ROWS)
    own_half = x3.at[z * NY + yh, own_rows]
    loads = [
        pltpu.make_async_copy(values, tiles.at[pl.ds(0, SLOTS)], local_sem.at[0]),
        pltpu.make_async_copy(feats.at[:, lanes], own_half, local_sem.at[1]),
        pltpu.make_async_copy(weight, wv, local_sem.at[2]),
        pltpu.make_async_copy(upstream, upv, local_sem.at[3]),
    ]

    peers = [at(dz=i) for i in (4, 3, 5, 2, 6, 1, 7)]
    peers += [at(dy=i, dc=k) for i in (2, 1, 3) for k in range(NC)] + [at(dc=1)]
    peers += [at(dr=i) for i in (6, 2, 5, 7, 3, 1, 4)]
    x, yl = rep % 4, rep // 4

    def target(dx, dyl):
        return lax.rem(yl + dyl, 2) * 4 + lax.rem(x + dx + 4, 4)

    near = ((1, 1), (-1, 1), (0, 1), (1, 0), (-1, 0))
    peers += [(at(dc=1)[0], target(dx, dyl)) for dx, dyl in near]
    barrier = pltpu.get_barrier_semaphore()
    for peer in peers:
        pl.semaphore_signal(barrier, inc=1, device_id=peer, device_id_type=MESH)
    for load in loads:
        load.start()
    pl.semaphore_wait(barrier, len(peers))

    def z_at(k):
        return lax.rem(z + k + NZ, NZ)

    def chip_block(k, jj):
        return x3.at[z_at(k) * NY + lax.rem(yh - jj + NY, NY)]

    y_in, up_in, down_in = {}, {}, {}

    step = 1 - 2 * c

    def send_up(s, jj):
        block = chip_block(step * (1 - s), jj)
        if s == 4:
            block = block.at[pl.ds(0, ROWS)]
        up_in[s, jj] = push(block, block, z_s.at[0, s, jj], z_r.at[0, s, jj], at(dz=step))

    def send_down(s, jj):
        block = chip_block(step * (s - 1), jj)
        if s == 4:
            block = block.at[pl.ds(ROWS, ROWS)]
        down_in[s, jj] = push(block, block, z_s.at[1, s, jj], z_r.at[1, s, jj], at(dz=-step))

    def send_ring(s, jj):
        send_up(s, jj)
        send_down(s, jj)

    def ring(s, jj):
        up_in[s, jj].wait_recv()
        if s < 4:
            send_up(s + 1, jj)
        down_in[s, jj].wait_recv()
        if s < 4:
            send_down(s + 1, jj)

    def from_y(jj):
        y_in[jj, 0].wait_recv()
        y_in[jj, 1].wait_recv()
        send_ring(1, jj)

    sib_own = push(feats.at[:, other_lanes], own_half, h_s.at[0], h_r.at[0], at(dc=1))
    for jj in (1, 3, 2):
        y_in[jj, 0] = push(feats.at[:, lanes], own_half, y_s.at[jj, 0], y_r.at[jj, 0], at(dy=jj))
        y_in[jj, 1] = push(feats.at[:, other_lanes], own_half, y_s.at[jj, 1], y_r.at[jj, 1], at(dy=jj, dc=1))
    tiles_in = push(values, tiles_sib.at[pl.ds(0, SLOTS)], h_s.at[1], h_r.at[1], at(dc=1))

    for load in small:
        load.wait()
    pos = to_column(trows[...] * COLS + tcols[...])
    live = iota((SLOTS, 1), 0) < tcount[0]
    hit = (pos == iota((SLOTS, TILE), 1)) & live
    info[...] = jnp.zeros_like(info)
    info[0:1] = SLOTS + jnp.sum(jnp.where(hit, iota((SLOTS, TILE), 0) - SLOTS, 0), axis=0, keepdims=True)
    info[1:2, 0:LAB] = lab[...]
    info_in = push(info, info_sib, h_s.at[2], h_r.at[2], at(dc=1))
    table_copy = pltpu.make_async_copy(info, table_s.at[0], local_sem.at[4])
    table_copy.start()

    loads[1].wait()
    sib_own.wait_recv()
    send_ring(1, 0)

    def picker(lab_row):
        lab_col = to_column(lab_row)
        twice = (lab_col == lab_row) & (iota((LAB, LAB), 1) < iota((LAB, LAB), 0))
        first = jnp.sum(jnp.where(twice, 1, 0), axis=1, keepdims=True) == 0
        return jnp.where((lab_col == iota((LAB, TEAM), 1)) & first, 1.0, 0.0).astype(BF16)

    pick = picker(lab[...])
    tiles[SLOTS] = jnp.zeros((TILE, TILE), BF16)
    tiles_sib[SLOTS] = jnp.zeros((TILE, TILE), BF16)

    def densify(team, held, nz):
        for j in range(NY):
            for rt in range(RT):
                slot = table_s[team, 0, rt * COLS + nz * NY + j]
                dense[team, nz, rt * TILE:(rt + 1) * TILE, j * TILE:(j + 1) * TILE] = held[slot]

    def densify_own(nz, carry):
        densify(0, tiles, nz)
        rows = jnp.dot(pick, dense[0, nz], preferred_element_type=F32).astype(BF16)
        for j in range(NY):
            asub[j, nz] = rows[:, j * TILE:(j + 1) * TILE]
        return carry

    def densify_sib(nz, carry):
        densify(1, tiles_sib, nz)
        return carry

    def add_block(k, fresh=False):
        nz = z_at(k)
        block = x3[pl.ds(nz * NY, NY)].reshape(NY * TILE, TILE)
        for team in range(NC):
            term = jnp.dot(dense[team, nz], block, preferred_element_type=F32)
            if fresh:
                acc[team] = term
            else:
                acc[team] += term

    loads[0].wait()
    table_copy.wait()
    lax.fori_loop(0, 4, densify_own, 0)
    from_y(1)
    from_y(3)
    ring(1, 0)
    from_y(2)
    lax.fori_loop(4, NZ, densify_own, 0)
    a_in = {}
    for jj in (2, 1, 3):
        a_in[jj] = push(asub.at[lax.rem(yh + jj, NY)], a4.at[yh], a_s.at[jj], a_r.at[jj], at(dy=jj))
    ring(1, 1)
    ring(1, 3)
    ring(2, 0)
    ring(1, 2)
    a4[yh] = asub[yh]
    info_in.wait_recv()
    sib_table = pltpu.make_async_copy(info_sib, table_s.at[1], local_sem.at[9])
    sib_table.start()
    pick_sib = picker(info_sib[1:2, 0:LAB])
    ring(2, 1)
    ring(2, 3)
    sib_table.wait()
    tiles_in.wait_recv()
    lax.fori_loop(0, 2, densify_sib, 0)
    ring(3, 0)
    ring(2, 2)
    lax.fori_loop(2, 5, densify_sib, 0)
    ring(3, 1)
    ring(3, 3)
    lax.fori_loop(5, NZ, densify_sib, 0)
    ring(3, 2)
    add_block(0, fresh=True)
    add_block(1)
    add_block(-1)
    add_block(2)
    add_block(-2)
    add_block(3)
    add_block(-3)
    for jj in (0, 1, 3, 2):
        ring(4, jj)
    add_block(4)

    for team, rows in enumerate((pick, pick_sib)):
        low = acc[team].astype(BF16)
        picked = jnp.dot(rows, low, preferred_element_type=F32).astype(BF16)
        base = team * REP_HALF
        for i in range(NR):
            stage[i, base:base + ROWS] = low[i * ROWS:(i + 1) * ROWS]
            stage[i, base + ROWS:base + REP_HALF] = picked
    halves = (pl.ds(0, REP_HALF), pl.ds(REP_HALF, REP_HALF))
    relay, rep_arrivals = {}, []
    for dyl in (1, 0):
        for side, dx in ((1, -1),):
            relay[side, dyl] = push(
                stage.at[target(2, dyl), halves[side]], relay_in.at[side, dyl],
                q_s.at[side, dyl], q_r.at[side, dyl], (loop, target(dx, 0)),
            )

    def send_rep(dx, dyl, side):
        to, slot = target(dx, dyl), dyl * 4 + dx + 1
        rep_arrivals.append(push(
            stage.at[to, halves[side]], rep_in.at[slot, :, lanes],
            rep_s.at[slot, side], rep_r.at[slot, side], (at(dc=side)[0], to),
        ))

    send_rep(2, 1, 0)
    send_rep(2, 0, 0)
    send_rep(0, 1, 0)
    send_rep(0, 1, 1)
    for dyl in (1, 0):
        for side, dx in enumerate((1, -1)):
            send_rep(dx, dyl, 1 - side)
        send_rep(1, dyl, 0)
    send_rep(0, 0, 1)
    rep_in[1, :, lanes] = stage[rep, 0:REP_HALF]
    for dyl in (1, 0):
        for side, dx in ((1, -1),):
            relay[side, dyl].wait_recv()
            to, part = target(dx, dyl), halves[side]
            merged = stage[to, part].astype(F32) + relay_in[side, dyl].astype(F32)
            stage[to, part] = merged.astype(BF16)
            send_rep(dx, dyl, side)
    gather_sends = list(sends)
    for jj in range(1, NY):
        a_in[jj].wait_recv()
    for i in range(NZ):
        block = jnp.concatenate([a4[j, i] for j in range(NY)], axis=0)
        at4[i] = block.astype(F32).T.astype(BF16)
    t_in = push(
        at4.at[:, pl.ds((1 - c) * ROWS, ROWS)], at8.at[:, :, pl.ds(c * TILE, TILE)],
        t_s.at[0], t_r.at[0], at(dc=1),
    )
    at8[:, :, pl.ds(pl.multiple_of(c * TILE, TILE), TILE)] = at4[:, pl.ds(pl.multiple_of(c * ROWS, ROWS), ROWS)]
    for copy in gather_sends:
        copy.wait_send()
    loads[2].wait()
    loads[3].wait()
    w = wv[...]
    up_lab = jnp.dot(pick, upv[...], preferred_element_type=F32)
    for copy in rep_arrivals:
        copy.wait_recv()
    total = rep_in[0].astype(F32)
    for i in (1, 2, 4, 5, 6):
        total += rep_in[i].astype(F32)
    total_v[...] = total
    total_v[:, lanes] += rep_in[3, :, lanes].astype(F32) + rep_in[7, :, lanes].astype(F32)
    total = total_v[...]
    agg = total.astype(BF16)
    pre = jnp.dot(agg, w, preferred_element_type=F32)
    gate = jax.nn.sigmoid(pre)
    layer_out[...] = (pre * gate)[0:ROWS].astype(BF16)
    pre_l, gate_l = pre[ROWS:], gate[ROWS:]
    slope = gate_l * (1.0 + pre_l * (1.0 - gate_l))
    mine = c * NY + yh
    msg[mine] = (up_lab * slope).astype(BF16)
    m_in, m_sib = {}, []
    for dy in (2, 1, 3):
        m_in[dy] = push(msg.at[mine], msg.at[mine], m_s.at[dy], m_r.at[dy], at(dy=dy))

    def pass_msg(dy):
        slot = msg.at[c * NY + lax.rem(yh - dy + NY, NY)]
        m_sib.append(push(slot, slot, m_s.at[4 + dy], m_r.at[4 + dy], at(dc=1)))

    pass_msg(0)
    chosen = (iota((FEAT, TILE), 0) == rep * LAB + iota((FEAT, TILE), 1)) & (iota((FEAT, TILE), 1) < LAB)
    chunk[c] = jnp.dot(agg[ROWS:], jnp.where(chosen, 1.0, 0.0).astype(BF16), preferred_element_type=F32).astype(BF16)
    chunk_in = push(chunk.at[c], chunk.at[c], m_s.at[0], m_r.at[0], at(dc=1))
    m_sib[0].wait_recv()
    chunk_in.wait_recv()
    part = lax.dot_general(
        chunk[...].reshape(NC * LAB, TILE), jnp.concatenate([msg[yh], msg[NY + yh]], axis=0),
        CONTRACT_ROWS, preferred_element_type=F32,
    )
    part_v[...] = part[0:LAB]
    wpart[z] = part_v[pl.ds(pl.multiple_of(c * HALF, HALF), HALF)].astype(BF16)
    w_in, u_in, b_in = [], [], []
    for d in (4, 3, 5, 2, 6, 1, 7):
        w_in.append(push(wpart.at[z], wpart.at[z], w_s.at[d], w_r.at[d], at(dz=d)))
    t_in.wait_recv()
    for dy in (1, 3, 2):
        m_in[dy].wait_recv()
        pass_msg(dy)
    for copy in m_sib[1:]:
        copy.wait_recv()

    grad_pre = msg[...].reshape(NC * NY * LAB, FEAT)
    for copy in reversed(w_in):
        copy.wait_recv()
    chunk_sum = wpart[0].astype(F32)
    for i in range(1, NZ):
        chunk_sum += wpart[i].astype(F32)
    ypart[yh, c] = chunk_sum.astype(BF16)
    for dy, dc in ((2, 1), (2, 0), (1, 1), (3, 1), (1, 0), (3, 0), (0, 1)):
        u_in.append(push(
            ypart.at[yh, c], ypart.at[yh, c], u_s.at[dc * NY + dy], u_r.at[dc * NY + dy], at(dy=dy, dc=dc)
        ))
    grad_agg = lax.dot_general(grad_pre, w, CONTRACT_LANES, preferred_element_type=F32).astype(BF16)
    term = jnp.dot(at8[...].reshape(NZ * ROWS, NC * NY * LAB), grad_agg, preferred_element_type=F32)
    cstage[...] = term.astype(BF16).reshape(NZ, ROWS, FEAT)
    top, bottom = pl.ds(0, ROWS // 2), pl.ds(ROWS // 2, ROWS // 2)
    far = [
        push(cstage.at[z_at(4), top], z_relay.at[0], f_s.at[0], f_r.at[0], at(dz=3)),
        push(cstage.at[z_at(4), bottom], z_relay.at[1], f_s.at[1], f_r.at[1], at(dz=-3)),
    ]
    for d in (2, -2, 3, -3):
        b_in.append(push(cstage.at[z_at(d)], cin.at[d % NZ], b_s.at[d % NZ], b_r.at[d % NZ], at(dz=d)))
    b_in.append(push(cstage.at[z_at(1), bottom], cin.at[1, bottom], b_s.at[1], b_r.at[1], at(dz=1)))
    b_in.append(push(cstage.at[z_at(-1), top], cin.at[7, top], b_s.at[7], b_r.at[7], at(dz=-1)))
    for copy in u_in:
        copy.wait_recv()
    chunk_sum = ypart[0].astype(F32)
    for i in range(1, NY):
        chunk_sum += ypart[i].astype(F32)
    gwbuf[rep] = chunk_sum.astype(BF16)
    v_in = []
    for d in (6, 2, 5, 7, 3, 1, 4):
        v_in.append(push(gwbuf.at[rep], gwbuf.at[rep], v_s.at[d], v_r.at[d], at(dr=d)))
    for i, (d, part) in enumerate(((1, top), (-1, bottom))):
        far[i].wait_recv()
        merged = cstage[z_at(d), part].astype(F32) + z_relay[i].astype(F32)
        cstage[z_at(d), part] = merged.astype(BF16)
        b_in.append(push(cstage.at[z_at(d), part], cin.at[d % NZ, part], f_s.at[2 + i], f_r.at[2 + i], at(dz=d)))
    total = cstage[z].astype(F32)
    for copy in b_in:
        copy.wait_recv()
    for d in (1, 2, 3, 5, 6, 7):
        total += cin[d].astype(F32)
    grad_feats[...] = total.astype(BF16)
    for copy in sends[len(gather_sends):]:
        copy.wait_send()
    for copy in reversed(v_in):
        copy.wait_recv()
    grad_weight[...] = gwbuf[...].astype(F32).reshape(FEAT, FEAT)


def write_out(layer_in, feats_in, weight_in, layer_out, grad_feats, grad_weight):
    layer_out[...] = layer_in[...]
    grad_feats[...] = feats_in[...]
    grad_weight[...] = weight_in[...]


def per_device(
    node_feats, weight_matrix, tile_values, tile_rows, tile_cols, tile_count, labelled, upstream
):
    hbm = pl.BlockSpec(memory_space=pl.ANY)
    vmem = pl.BlockSpec(memory_space=pltpu.VMEM)
    dma = pltpu.SemaphoreType.DMA
    shapes = (
        jax.ShapeDtypeStruct((ROWS, FEAT), BF16),
        jax.ShapeDtypeStruct((ROWS, FEAT), BF16),
        jax.ShapeDtypeStruct((FEAT, FEAT), F32),
    )
    results = pl.pallas_call(
        kernel,
        name="graph_layer",
        out_shape=shapes,
        in_specs=[hbm] * 8,
        out_specs=(vmem, vmem, vmem),
        scratch_shapes=[
            pltpu.VMEM((COLS, TILE, TILE), BF16),
            pltpu.VMEM((SLOTS + 1, TILE, TILE), BF16),
            pltpu.VMEM((SLOTS + 1, TILE, TILE), BF16),
            pltpu.VMEM((NC, NZ, TEAM, NY * TILE), BF16),
            pltpu.VMEM((FEAT, FEAT), BF16),
            pltpu.VMEM((TEAM, FEAT), BF16),
            pltpu.VMEM((1, SLOTS), I32),
            pltpu.VMEM((1, SLOTS), I32),
            pltpu.VMEM((1, LAB), I32),
            pltpu.SMEM((1,), I32),
            pltpu.VMEM((8, TILE), I32),
            pltpu.VMEM((8, TILE), I32),
            pltpu.SMEM((NC, 8, TILE), I32),
            pltpu.VMEM((NC, TEAM, TILE), F32),
            pltpu.VMEM((NY, NZ, LAB, TILE), BF16),
            pltpu.VMEM((NY, NZ, LAB, TILE), BF16),
            pltpu.VMEM((NZ, TILE, TILE), BF16),
            pltpu.VMEM((NZ, ROWS, NC * TILE), BF16),
            pltpu.VMEM((NR, NC * REP_HALF, TILE), BF16),
            pltpu.VMEM((8, REP_HALF, FEAT), BF16),
            pltpu.VMEM((REP_HALF, FEAT), F32),
            pltpu.VMEM((2, 2, REP_HALF, TILE), BF16),
            pltpu.VMEM((NC * NY, LAB, FEAT), BF16),
            pltpu.VMEM((NC, LAB, TILE), BF16),
            pltpu.VMEM((NZ, HALF, FEAT), BF16),
            pltpu.VMEM((NY, NC, HALF, FEAT), BF16),
            pltpu.VMEM((LAB, FEAT), F32),
            pltpu.VMEM((NZ, ROWS, FEAT), BF16),
            pltpu.VMEM((NZ, ROWS, FEAT), BF16),
            pltpu.VMEM((NR, NC, HALF, FEAT), BF16),
            pltpu.VMEM((2, ROWS // 2, FEAT), BF16),
            dma((10,)),
            dma((4, 2)), dma((4, 2)), dma((4,)), dma((4,)), dma((2, 5, 4)), dma((2, 5, 4)),
            dma((4,)), dma((4,)), dma((1,)), dma((1,)),
            dma((2, 2)), dma((2, 2)), dma((8, 2)), dma((8, 2)), dma((8,)), dma((8,)), dma((8,)), dma((8,)), dma((8,)), dma((8,)),
            dma((8,)), dma((8,)), dma((4,)), dma((4,)), dma((8,)), dma((8,)),
        ],
        compiler_params=pltpu.CompilerParams(
            collective_id=0, has_side_effects=True, vmem_limit_bytes=60 * 2**20
        ),
    )(
        node_feats, weight_matrix, tile_values, tile_rows.reshape(1, SLOTS), tile_cols.reshape(1, SLOTS),
        tile_count, labelled, upstream,
    )
    return pl.pallas_call(
        write_out,
        name="write_out",
        out_shape=shapes,
        in_specs=[vmem] * 3,
        out_specs=(vmem,) * 3,
        compiler_params=pltpu.CompilerParams(vmem_limit_bytes=60 * 2**20),
    )(*results)


def solution(mesh):
    placed = (
        P(("loop", "rep"), None),
        P(),
        P(("loop", "rep"), None, None),
        P(("loop", "rep")),
        P(("loop", "rep")),
        P(("loop", "rep")),
        P("loop", None),
        P("loop", None),
    )
    return jax.shard_map(
        per_device,
        mesh=mesh,
        in_specs=placed,
        out_specs=(P(("loop", "rep"), None), P(("loop", "rep"), None), P()),
        check_vma=False,
    )
```

```python
import jax
import jax.numpy as jnp
from jax import lax
from jax.experimental import pallas as pl
from jax.experimental.pallas import tpu as pltpu
from jax.sharding import PartitionSpec as P

MESH = pl.DeviceIdType.MESH
NZ, NY, NC, NR = 8, 4, 2, 8
ROWS, FEAT, TILE, SLOTS = 64, 256, 128, 64
TEAM, LAB, RT = 512, 32, 4
REP_HALF = ROWS + LAB
HALF = LAB // NC
COLS = NZ * NY
F32, BF16, I32 = jnp.float32, jnp.bfloat16, jnp.int32
CONTRACT_ROWS = (((0,), (0,)), ((), ()))
CONTRACT_LANES = (((1,), (1,)), ((), ()))


def iota(shape, dim):
    return lax.broadcasted_iota(I32, shape, dim)


def to_column(row):
    n = row.shape[1]
    square = jnp.broadcast_to(row, (n, n))
    return jnp.sum(jnp.where(iota((n, n), 0) == iota((n, n), 1), square, 0), axis=1, keepdims=True)


def kernel(
    feats, weight, values, trows_h, tcols_h, tcount_h, lab_h, upstream,
    layer_out, grad_feats, grad_weight,
    x3, tiles, tiles_sib, dense, wv, upv, trows, tcols, lab, tcount, info, info_sib, table_s, acc, asub, a4, at4, at8,
    stage, rep_in, total_v, relay_in, msg, chunk, wpart, ypart, part_v, cstage, cin, gwbuf, z_relay,
    local_sem, y_s, y_r, h_s, h_r, z_s, z_r, a_s, a_r, t_s, t_r,
    q_s, q_r, rep_s, rep_r, m_s, m_r, w_s, w_r, u_s, u_r, b_s, b_r, f_s, f_r, v_s, v_r,
):
    loop, rep = lax.axis_index("loop"), lax.axis_index("rep")
    z, yh, c = loop // 8, (loop // 2) % 4, loop % 2

    def at(dz=0, dy=0, dc=0, dr=0):
        nz, ny = lax.rem(z + dz + NZ, NZ), lax.rem(yh + dy + NY, NY)
        nc, nr = lax.rem(c + dc, NC), lax.rem(rep + dr, NR)
        return (nz * 8 + ny * 2 + nc, nr)

    sends = []

    def push(src, dst, ss, rs, to):
        copy = pltpu.make_async_remote_copy(
            src_ref=src, dst_ref=dst, send_sem=ss, recv_sem=rs, device_id=to, device_id_type=MESH
        )
        copy.start()
        sends.append(copy)
        return copy

    small = [
        pltpu.make_async_copy(trows_h, trows, local_sem.at[5]),
        pltpu.make_async_copy(tcols_h, tcols, local_sem.at[6]),
        pltpu.make_async_copy(tcount_h, tcount, local_sem.at[7]),
        pltpu.make_async_copy(lab_h, lab, local_sem.at[8]),
    ]
    for load in small:
        load.start()
    lanes = pl.ds(pl.multiple_of(c * TILE, TILE), TILE)
    other_lanes = pl.ds(pl.multiple_of((1 - c) * TILE, TILE), TILE)
    own_rows = pl.ds(pl.multiple_of(c * ROWS, ROWS), ROWS)
    own_half = x3.at[z * NY + yh, own_rows]
    loads = [
        pltpu.make_async_copy(values, tiles.at[pl.ds(0, SLOTS)], local_sem.at[0]),
        pltpu.make_async_copy(feats.at[:, lanes], own_half, local_sem.at[1]),
        pltpu.make_async_copy(weight, wv, local_sem.at[2]),
        pltpu.make_async_copy(upstream, upv, local_sem.at[3]),
    ]

    peers = [at(dz=i) for i in (4, 3, 5, 2, 6, 1, 7)]
    peers += [at(dy=i, dc=k) for i in (2, 1, 3) for k in range(NC)] + [at(dc=1)]
    peers += [at(dr=i) for i in (6, 2, 5, 7, 3, 1, 4)]
    x, yl = rep % 4, rep // 4

    def target(dx, dyl):
        return lax.rem(yl + dyl, 2) * 4 + lax.rem(x + dx + 4, 4)

    near = ((1, 1), (-1, 1), (0, 1), (1, 0), (-1, 0))
    peers += [(at(dc=1)[0], target(dx, dyl)) for dx, dyl in near]
    barrier = pltpu.get_barrier_semaphore()
    for peer in peers:
        pl.semaphore_signal(barrier, inc=1, device_id=peer, device_id_type=MESH)
    for load in loads:
        load.start()
    pl.semaphore_wait(barrier, len(peers))

    def z_at(k):
        return lax.rem(z + k + NZ, NZ)

    def chip_block(k, jj):
        return x3.at[z_at(k) * NY + lax.rem(yh - jj + NY, NY)]

    y_in, up_in, down_in = {}, {}, {}

    step = 1 - 2 * c

    def send_up(s, jj):
        block = chip_block(step * (1 - s), jj)
        if s == 4:
            block = block.at[pl.ds(0, ROWS)]
        up_in[s, jj] = push(block, block, z_s.at[0, s, jj], z_r.at[0, s, jj], at(dz=step))

    def send_down(s, jj):
        block = chip_block(step * (s - 1), jj)
        if s == 4:
            block = block.at[pl.ds(ROWS, ROWS)]
        down_in[s, jj] = push(block, block, z_s.at[1, s, jj], z_r.at[1, s, jj], at(dz=-step))

    def send_ring(s, jj):
        send_up(s, jj)
        send_down(s, jj)

    def ring(s, jj):
        up_in[s, jj].wait_recv()
        if s < 4:
            send_up(s + 1, jj)
        down_in[s, jj].wait_recv()
        if s < 4:
            send_down(s + 1, jj)

    def from_y(jj):
        y_in[jj, 0].wait_recv()
        y_in[jj, 1].wait_recv()
        send_ring(1, jj)

    sib_own = push(feats.at[:, other_lanes], own_half, h_s.at[0], h_r.at[0], at(dc=1))
    for jj in (1, 3, 2):
        y_in[jj, 0] = push(feats.at[:, lanes], own_half, y_s.at[jj, 0], y_r.at[jj, 0], at(dy=jj))
        y_in[jj, 1] = push(feats.at[:, other_lanes], own_half, y_s.at[jj, 1], y_r.at[jj, 1], at(dy=jj, dc=1))
    tiles_in = push(values, tiles_sib.at[pl.ds(0, SLOTS)], h_s.at[1], h_r.at[1], at(dc=1))

    for load in small:
        load.wait()
    pos = to_column(trows[...] * COLS + tcols[...])
    live = iota((SLOTS, 1), 0) < tcount[0]
    hit = (pos == iota((SLOTS, TILE), 1)) & live
    info[...] = jnp.zeros_like(info)
    info[0:1] = SLOTS + jnp.sum(jnp.where(hit, iota((SLOTS, TILE), 0) - SLOTS, 0), axis=0, keepdims=True)
    info[1:2, 0:LAB] = lab[...]
    info_in = push(info, info_sib, h_s.at[2], h_r.at[2], at(dc=1))
    table_copy = pltpu.make_async_copy(info, table_s.at[0], local_sem.at[4])
    table_copy.start()

    loads[1].wait()
    sib_own.wait_recv()
    send_ring(1, 0)

    def picker(lab_row):
        lab_col = to_column(lab_row)
        twice = (lab_col == lab_row) & (iota((LAB, LAB), 1) < iota((LAB, LAB), 0))
        first = jnp.sum(jnp.where(twice, 1, 0), axis=1, keepdims=True) == 0
        return jnp.where((lab_col == iota((LAB, TEAM), 1)) & first, 1.0, 0.0).astype(BF16)

    pick = picker(lab[...])
    tiles[SLOTS] = jnp.zeros((TILE, TILE), BF16)
    tiles_sib[SLOTS] = jnp.zeros((TILE, TILE), BF16)

    def densify(team, held, nz):
        for j in range(NY):
            for rt in range(RT):
                slot = table_s[team, 0, rt * COLS + nz * NY + j]
                dense[team, nz, rt * TILE:(rt + 1) * TILE, j * TILE:(j + 1) * TILE] = held[slot]

    def densify_own(nz, carry):
        densify(0, tiles, nz)
        rows = jnp.dot(pick, dense[0, nz], preferred_element_type=F32).astype(BF16)
        for j in range(NY):
            asub[j, nz] = rows[:, j * TILE:(j + 1) * TILE]
        return carry

    def densify_sib(nz, carry):
        densify(1, tiles_sib, nz)
        return carry

    def add_block(k, fresh=False):
        nz = z_at(k)
        block = x3[pl.ds(nz * NY, NY)].reshape(NY * TILE, TILE)
        for team in range(NC):
            term = jnp.dot(dense[team, nz], block, preferred_element_type=F32)
            if fresh:
                acc[team] = term
            else:
                acc[team] += term

    loads[0].wait()
    table_copy.wait()
    lax.fori_loop(0, 4, densify_own, 0)
    from_y(1)
    from_y(3)
    ring(1, 0)
    from_y(2)
    lax.fori_loop(4, NZ, densify_own, 0)
    a_in = {}
    for jj in (2, 1, 3):
        a_in[jj] = push(asub.at[lax.rem(yh + jj, NY)], a4.at[yh], a_s.at[jj], a_r.at[jj], at(dy=jj))
    ring(1, 1)
    ring(1, 3)
    ring(2, 0)
    ring(1, 2)
    a4[yh] = asub[yh]
    info_in.wait_recv()
    sib_table = pltpu.make_async_copy(info_sib, table_s.at[1], local_sem.at[9])
    sib_table.start()
    pick_sib = picker(info_sib[1:2, 0:LAB])
    ring(2, 1)
    ring(2, 3)
    sib_table.wait()
    tiles_in.wait_recv()
    lax.fori_loop(0, 2, densify_sib, 0)
    ring(3, 0)
    ring(2, 2)
    lax.fori_loop(2, 5, densify_sib, 0)
    ring(3, 1)
    ring(3, 3)
    lax.fori_loop(5, NZ, densify_sib, 0)
    ring(3, 2)
    add_block(0, fresh=True)
    add_block(1)
    add_block(-1)
    add_block(2)
    add_block(-2)
    add_block(3)
    add_block(-3)
    for jj in (0, 1, 3, 2):
        ring(4, jj)
    add_block(4)

    for team, rows in enumerate((pick, pick_sib)):
        low = acc[team].astype(BF16)
        picked = jnp.dot(rows, low, preferred_element_type=F32).astype(BF16)
        base = team * REP_HALF
        for i in range(NR):
            stage[i, base:base + ROWS] = low[i * ROWS:(i + 1) * ROWS]
            stage[i, base + ROWS:base + REP_HALF] = picked
    halves = (pl.ds(0, REP_HALF), pl.ds(REP_HALF, REP_HALF))
    rep_arrivals = []

    def send_rep(dx, dyl, side):
        to, slot = target(dx, dyl), dyl * 4 + dx + 1
        rep_arrivals.append(push(
            stage.at[to, halves[side]], rep_in.at[slot, :, lanes],
            rep_s.at[slot, side], rep_r.at[slot, side], (at(dc=side)[0], to),
        ))

    for dx, dyl in ((2, 1), (2, 0), (1, 1), (-1, 1), (0, 1), (1, 0), (-1, 0)):
        for side in range(NC):
            send_rep(dx, dyl, side)
    send_rep(0, 0, 1)
    rep_in[1, :, lanes] = stage[rep, 0:REP_HALF]
    gather_sends = list(sends)
    for jj in range(1, NY):
        a_in[jj].wait_recv()
    for i in range(NZ):
        block = jnp.concatenate([a4[j, i] for j in range(NY)], axis=0)
        at4[i] = block.astype(F32).T.astype(BF16)
    t_in = push(
        at4.at[:, pl.ds((1 - c) * ROWS, ROWS)], at8.at[:, :, pl.ds(c * TILE, TILE)],
        t_s.at[0], t_r.at[0], at(dc=1),
    )
    at8[:, :, pl.ds(pl.multiple_of(c * TILE, TILE), TILE)] = at4[:, pl.ds(pl.multiple_of(c * ROWS, ROWS), ROWS)]
    for copy in gather_sends:
        copy.wait_send()
    loads[2].wait()
    loads[3].wait()
    w = wv[...]
    up_lab = jnp.dot(pick, upv[...], preferred_element_type=F32)
    for copy in rep_arrivals:
        copy.wait_recv()
    total = rep_in[0].astype(F32)
    for i in range(1, 8):
        total += rep_in[i].astype(F32)
    agg = total.astype(BF16)
    pre = jnp.dot(agg, w, preferred_element_type=F32)
    gate = jax.nn.sigmoid(pre)
    layer_out[...] = (pre * gate)[0:ROWS].astype(BF16)
    pre_l, gate_l = pre[ROWS:], gate[ROWS:]
    slope = gate_l * (1.0 + pre_l * (1.0 - gate_l))
    mine = c * NY + yh
    msg[mine] = (up_lab * slope).astype(BF16)
    m_in, m_sib = {}, []
    for dy in (2, 1, 3):
        m_in[dy] = push(msg.at[mine], msg.at[mine], m_s.at[dy], m_r.at[dy], at(dy=dy))

    def pass_msg(dy):
        slot = msg.at[c * NY + lax.rem(yh - dy + NY, NY)]
        m_sib.append(push(slot, slot, m_s.at[4 + dy], m_r.at[4 + dy], at(dc=1)))

    pass_msg(0)
    chosen = (iota((FEAT, TILE), 0) == rep * LAB + iota((FEAT, TILE), 1)) & (iota((FEAT, TILE), 1) < LAB)
    chunk[c] = jnp.dot(agg[ROWS:], jnp.where(chosen, 1.0, 0.0).astype(BF16), preferred_element_type=F32).astype(BF16)
    chunk_in = push(chunk.at[c], chunk.at[c], m_s.at[0], m_r.at[0], at(dc=1))
    m_sib[0].wait_recv()
    chunk_in.wait_recv()
    part = lax.dot_general(
        chunk[...].reshape(NC * LAB, TILE), jnp.concatenate([msg[yh], msg[NY + yh]], axis=0),
        CONTRACT_ROWS, preferred_element_type=F32,
    )
    part_v[...] = part[0:LAB]
    wpart[z] = part_v[pl.ds(pl.multiple_of(c * HALF, HALF), HALF)].astype(BF16)
    w_in, u_in, b_in = [], [], []
    for d in (4, 3, 5, 2, 6, 1, 7):
        w_in.append(push(wpart.at[z], wpart.at[z], w_s.at[d], w_r.at[d], at(dz=d)))
    t_in.wait_recv()
    for dy in (1, 3, 2):
        m_in[dy].wait_recv()
        pass_msg(dy)
    for copy in m_sib[1:]:
        copy.wait_recv()

    grad_pre = msg[...].reshape(NC * NY * LAB, FEAT)
    for copy in reversed(w_in):
        copy.wait_recv()
    chunk_sum = wpart[0].astype(F32)
    for i in range(1, NZ):
        chunk_sum += wpart[i].astype(F32)
    ypart[yh, c] = chunk_sum.astype(BF16)
    for dy, dc in ((2, 1), (2, 0), (1, 1), (3, 1), (1, 0), (3, 0), (0, 1)):
        u_in.append(push(
            ypart.at[yh, c], ypart.at[yh, c], u_s.at[dc * NY + dy], u_r.at[dc * NY + dy], at(dy=dy, dc=dc)
        ))
    grad_agg = lax.dot_general(grad_pre, w, CONTRACT_LANES, preferred_element_type=F32).astype(BF16)
    term = jnp.dot(at8[...].reshape(NZ * ROWS, NC * NY * LAB), grad_agg, preferred_element_type=F32)
    cstage[...] = term.astype(BF16).reshape(NZ, ROWS, FEAT)
    for d in (1, 7, 2, 6, 3, 5, 4):
        b_in.append(push(cstage.at[z_at(d)], cin.at[d], b_s.at[d], b_r.at[d], at(dz=d)))
    for copy in u_in:
        copy.wait_recv()
    chunk_sum = ypart[0].astype(F32)
    for i in range(1, NY):
        chunk_sum += ypart[i].astype(F32)
    gwbuf[rep] = chunk_sum.astype(BF16)
    v_in = []
    for d in (6, 2, 5, 7, 3, 1, 4):
        v_in.append(push(gwbuf.at[rep], gwbuf.at[rep], v_s.at[d], v_r.at[d], at(dr=d)))
    total = cstage[z].astype(F32)
    for copy in b_in:
        copy.wait_recv()
    for d in range(1, NZ):
        total += cin[d].astype(F32)
    grad_feats[...] = total.astype(BF16)
    for copy in sends[len(gather_sends):]:
        copy.wait_send()
    for copy in reversed(v_in):
        copy.wait_recv()
    grad_weight[...] = gwbuf[...].astype(F32).reshape(FEAT, FEAT)


def write_out(layer_in, feats_in, weight_in, layer_out, grad_feats, grad_weight):
    layer_out[...] = layer_in[...]
    grad_feats[...] = feats_in[...]
    grad_weight[...] = weight_in[...]


def per_device(
    node_feats, weight_matrix, tile_values, tile_rows, tile_cols, tile_count, labelled, upstream
):
    hbm = pl.BlockSpec(memory_space=pl.ANY)
    vmem = pl.BlockSpec(memory_space=pltpu.VMEM)
    dma = pltpu.SemaphoreType.DMA
    shapes = (
        jax.ShapeDtypeStruct((ROWS, FEAT), BF16),
        jax.ShapeDtypeStruct((ROWS, FEAT), BF16),
        jax.ShapeDtypeStruct((FEAT, FEAT), F32),
    )
    results = pl.pallas_call(
        kernel,
        name="graph_layer",
        out_shape=shapes,
        in_specs=[hbm] * 8,
        out_specs=(vmem, vmem, vmem),
        scratch_shapes=[
            pltpu.VMEM((COLS, TILE, TILE), BF16),
            pltpu.VMEM((SLOTS + 1, TILE, TILE), BF16),
            pltpu.VMEM((SLOTS + 1, TILE, TILE), BF16),
            pltpu.VMEM((NC, NZ, TEAM, NY * TILE), BF16),
            pltpu.VMEM((FEAT, FEAT), BF16),
            pltpu.VMEM((TEAM, FEAT), BF16),
            pltpu.VMEM((1, SLOTS), I32),
            pltpu.VMEM((1, SLOTS), I32),
            pltpu.VMEM((1, LAB), I32),
            pltpu.SMEM((1,), I32),
            pltpu.VMEM((8, TILE), I32),
            pltpu.VMEM((8, TILE), I32),
            pltpu.SMEM((NC, 8, TILE), I32),
            pltpu.VMEM((NC, TEAM, TILE), F32),
            pltpu.VMEM((NY, NZ, LAB, TILE), BF16),
            pltpu.VMEM((NY, NZ, LAB, TILE), BF16),
            pltpu.VMEM((NZ, TILE, TILE), BF16),
            pltpu.VMEM((NZ, ROWS, NC * TILE), BF16),
            pltpu.VMEM((NR, NC * REP_HALF, TILE), BF16),
            pltpu.VMEM((8, REP_HALF, FEAT), BF16),
            pltpu.VMEM((REP_HALF, FEAT), F32),
            pltpu.VMEM((2, 2, REP_HALF, TILE), BF16),
            pltpu.VMEM((NC * NY, LAB, FEAT), BF16),
            pltpu.VMEM((NC, LAB, TILE), BF16),
            pltpu.VMEM((NZ, HALF, FEAT), BF16),
            pltpu.VMEM((NY, NC, HALF, FEAT), BF16),
            pltpu.VMEM((LAB, FEAT), F32),
            pltpu.VMEM((NZ, ROWS, FEAT), BF16),
            pltpu.VMEM((NZ, ROWS, FEAT), BF16),
            pltpu.VMEM((NR, NC, HALF, FEAT), BF16),
            pltpu.VMEM((2, ROWS // 2, FEAT), BF16),
            dma((10,)),
            dma((4, 2)), dma((4, 2)), dma((4,)), dma((4,)), dma((2, 5, 4)), dma((2, 5, 4)),
            dma((4,)), dma((4,)), dma((1,)), dma((1,)),
            dma((2, 2)), dma((2, 2)), dma((8, 2)), dma((8, 2)), dma((8,)), dma((8,)), dma((8,)), dma((8,)), dma((8,)), dma((8,)),
            dma((8,)), dma((8,)), dma((4,)), dma((4,)), dma((8,)), dma((8,)),
        ],
        compiler_params=pltpu.CompilerParams(
            collective_id=0, has_side_effects=True, vmem_limit_bytes=60 * 2**20
        ),
    )(
        node_feats, weight_matrix, tile_values, tile_rows.reshape(1, SLOTS), tile_cols.reshape(1, SLOTS),
        tile_count, labelled, upstream,
    )
    return pl.pallas_call(
        write_out,
        name="write_out",
        out_shape=shapes,
        in_specs=[vmem] * 3,
        out_specs=(vmem,) * 3,
        compiler_params=pltpu.CompilerParams(vmem_limit_bytes=60 * 2**20),
    )(*results)


def solution(mesh):
    placed = (
        P(("loop", "rep"), None),
        P(),
        P(("loop", "rep"), None, None),
        P(("loop", "rep")),
        P(("loop", "rep")),
        P(("loop", "rep")),
        P("loop", None),
        P("loop", None),
    )
    return jax.shard_map(
        per_device,
        mesh=mesh,
        in_specs=placed,
        out_specs=(P(("loop", "rep"), None), P(("loop", "rep"), None), P()),
        check_vma=False,
    )
```
